32 devices in a mesh: section: 8 (over z, core), expert: 4 (over y, x).
Axes of the slice: x: 2, y: 2, z: 4, core: 2. Of those that a mesh axis runs over, the one named last changes fastest.
Arguments:
- tokens: bfloat16 [256, 3072], P(('section', 'expert')), may hold values from -6 to 6
- upstream: bfloat16 [256, 3072], P(('section', 'expert')), may hold values from -2 to 2
- route_ids: int32 [256, 2], P(('section', 'expert')), may hold values from 0 to 3, all different within a row; in each aligned block of 8 rows (0 to 7, 8 to 15, ...) at most 8 rows name the same one
- route_gates: bfloat16 [256, 2], P(('section', 'expert')), may hold values from 0.099609375 to 0.8984375
- w_gate: bfloat16 [4, 3072, 2048], P('expert', None, 'section'), may hold values from -0.109375 to 0.109375
- w_up: bfloat16 [4, 3072, 2048], P('expert', None, 'section'), may hold values from -0.109375 to 0.109375
- w_down: bfloat16 [4, 2048, 3072], P('expert', 'section'), may hold values from -0.125 to 0.125
Outputs:
- grad_tokens: bfloat16 [256, 3072], P(('section', 'expert'))
- grad_gates: float32 [256, 2], P(('section', 'expert'))
- grad_w_gate: bfloat16 [4, 3072, 2048], P('expert', None, 'section')
- grad_w_up: bfloat16 [4, 3072, 2048], P('expert', None, 'section')
- grad_w_down: bfloat16 [4, 2048, 3072], P('expert', 'section')
The draws below stay inside these ranges and needn't reach their ends.
Inputs may be any that keep to these rules, and one draw needn't show every extreme that they name: `route_ids`: the two experts of a token differ. Among the 16 choices of the tokens of one device, each expert is named at most 8 times, and in some device's tokens some expert is named exactly 8 times.
All inputs are finite; a program needn't handle non-finite values.
Results may differ from the reference program's by a relative error of at most 0.0058.
Values may be sent and summed in bfloat16 or wider, within the bound.
No kernel may reach another device: no remote copies, remote signals or barrier semaphores. Data moves between devices by JAX's collectives and lax.ppermute only.
A program may use at most 128 MiB of HBM per device.

```python
import math
import jax
import jax.numpy as jnp
import numpy as np
from jax import lax

D = 3072
TOK_DEV = 8
EXPERTS = 4
CAP = 8
F = 2048
TOKENS = 256


def level_of(rng, dims, split, low, top_value):
    loudness, own = 1.0, jax.random.fold_in(rng, 6)
    for dim, parts in split:
        draws = jnp.exp(jax.random.uniform(jax.random.fold_in(own, dim), (parts,), jnp.float32, low / len(split), top_value / len(split)))
        loudness = loudness * jnp.repeat(draws, dims[dim] // parts).reshape([-1 if axis == dim else 1 for axis in range(len(dims))])
    return loudness


def shared_out(own_key, own, number, rows, count, top, reach, lean):
    sequence = jax.random.permutation(own_key, count)
    heavy_load, usual = portions_of(count, rows * top, reach, lean, True), portions_of(count, rows * top, reach, lean, False)
    places = jnp.arange(count)

    def named(tallies, turn):
        used = int((tallies > 0).sum())
        fixed = max(1, used // 4)
        shifted = fixed + (places - fixed + turn * (used - fixed)) % max(1, count - fixed)
        return jnp.zeros((count,), jnp.int32).at[sequence[jnp.where(places < fixed, places, shifted)]].set(jnp.asarray(tallies, jnp.int32))

    tallies = jnp.where(number % 4 == 0, named(heavy_load, number // 4), named(usual, number - number // 4 - 1))
    mixed = jax.random.permutation(jax.random.fold_in(own, 3), count)
    source_of, receiver = mixed[0:count // 2 * 2:2], mixed[1:count // 2 * 2:2]
    slack = jnp.minimum(tallies[source_of] - 1, reach - tallies[receiver]) // 2
    slack = jnp.where((source_of == sequence[0]) | (receiver == sequence[0]) | (tallies[receiver] == 0), 0, jnp.maximum(slack, 0))
    shifted = jax.random.randint(jax.random.fold_in(own, 4), (count // 2,), 0, 1 << 20) % (slack + 1)
    tallies = tallies.at[source_of].add(-shifted).at[receiver].add(shifted)
    items = jnp.searchsorted(jnp.cumsum(tallies), jnp.arange(rows * top), side="right").astype(jnp.int32)
    table = items.reshape(top, rows).T
    table = table[jax.random.permutation(jax.random.fold_in(own, 1), rows)]
    turn = jax.random.randint(jax.random.fold_in(own, 2), (rows, 1), 0, top)
    return jnp.take_along_axis(table, (jnp.arange(top)[None, :] + turn) % top, axis=1)


def portions_of(number_of, total, reach, lean, full):
    portions = [(1 << 20) // math.isqrt(standing ** lean) + 1 for standing in range(1, number_of + 1)]
    largest = reach if full else min(reach, max(-(-total // number_of), total * portions[0] // sum(portions)))
    least = 1 if total - largest >= number_of - 1 else 0
    holding, spare = [largest] + [least] * (number_of - 1), total - largest - least * (number_of - 1)
    while spare > 0:
        free = [i for i in range(1, number_of) if holding[i] < largest] or [i for i in range(1, number_of) if holding[i] < reach]
        whole, left = sum([portions[i] for i in free]), spare
        for i in free:
            addition = min(reach - holding[i], max(1, left * portions[i] // whole), spare)
            holding[i] = holding[i] + addition
            spare = spare - addition
    return np.array(holding)


def bell_draw(own_key, shape, deviation, reach, pieces=(), kind=jnp.bfloat16):
    entries = deviation * jax.random.normal(own_key, shape, jnp.float32)
    if pieces:
        entries = entries * level_of(own_key, shape, pieces, -0.22, 0.18)
    return jnp.clip(entries, -reach, reach).astype(kind)


def setup_inputs(seed: int = 0) -> dict:
    seeds = jax.random.split(jax.random.key(seed), 8)
    tokens = bell_draw(seeds[0], (TOKENS, D), 1.0, 6.0, ((0, 32),))
    upstream = bell_draw(seeds[1], (TOKENS, D), 0.3, 2.0, ((0, 32),))
    route_ids_keys = jax.random.split(jax.random.fold_in(seeds[2], 1), TOKENS // TOK_DEV)
    route_ids_turns = jax.random.permutation(jax.random.fold_in(seeds[2], 3), TOKENS // TOK_DEV)
    route_ids = jax.vmap(lambda own, number: shared_out(jax.random.fold_in(seeds[2], 2), own, number, TOK_DEV, EXPERTS, 2, CAP, 2))(route_ids_keys, route_ids_turns).reshape((TOKENS, 2))
    route_gates = jnp.clip(0.099609375 + 0.7988281 * jax.random.uniform(seeds[3], (TOKENS, 2), jnp.float32) ** level_of(seeds[3], (TOKENS, 2), ((0, 32),), -0.2, 0.2), 0.099609375, 0.8984375).astype(jnp.bfloat16)
    w_gate = bell_draw(seeds[4], (EXPERTS, D, F), D ** -0.5, 0.109375, ((0, 4), (2, 8)))
    w_up = bell_draw(seeds[5], (EXPERTS, D, F), D ** -0.5, 0.109375, ((0, 4), (2, 8)))
    w_down = bell_draw(seeds[6], (EXPERTS, F, D), F ** -0.5, 0.125, ((0, 4), (1, 8)))
    return dict(tokens=tokens, upstream=upstream, route_ids=route_ids, route_gates=route_gates, w_gate=w_gate, w_up=w_up, w_down=w_down)


def one_expert(operands):
    rows_x, rows_dy, rows_weight, gate_slab, up_slab, down_slab = operands
    pre_gate = jnp.dot(rows_x, gate_slab, preferred_element_type=jnp.float32)
    pre_up = jnp.dot(rows_x, up_slab, preferred_element_type=jnp.float32)
    sigmoid_gate = jax.nn.sigmoid(pre_gate)
    active = pre_gate * sigmoid_gate
    hidden = (active * pre_up).astype(jnp.bfloat16)
    expert_out = jnp.dot(hidden, down_slab, preferred_element_type=jnp.float32)
    gate_grad = jnp.sum(rows_dy.astype(jnp.float32) * expert_out, axis=1)
    back_proj = jnp.dot(rows_dy, down_slab.T, preferred_element_type=jnp.float32)
    weight = rows_weight[:, None]
    d_hidden = weight * back_proj
    d_gate = (d_hidden * pre_up * (sigmoid_gate * (1.0 + pre_gate * (1.0 - sigmoid_gate)))).astype(jnp.bfloat16)
    d_up = (d_hidden * active).astype(jnp.bfloat16)
    scaled_up = (weight * rows_dy.astype(jnp.float32)).astype(jnp.bfloat16)
    grad_down = jnp.dot(hidden.T, scaled_up, preferred_element_type=jnp.float32).astype(jnp.bfloat16)
    grad_gate = jnp.dot(rows_x.T, d_gate, preferred_element_type=jnp.float32).astype(jnp.bfloat16)
    grad_up = jnp.dot(rows_x.T, d_up, preferred_element_type=jnp.float32).astype(jnp.bfloat16)
    grad_rows = jnp.dot(d_gate, gate_slab.T, preferred_element_type=jnp.float32) + jnp.dot(d_up, up_slab.T, preferred_element_type=jnp.float32)
    return grad_rows, gate_grad, grad_gate, grad_up, grad_down


def reference(tokens, upstream, route_ids, route_gates, w_gate, w_up, w_down):
    blocks = TOKENS // TOK_DEV
    flattened = route_ids.reshape(blocks, 2 * TOK_DEV).astype(jnp.int32)
    onehot = (flattened[:, :, None] == jnp.arange(EXPERTS, dtype=jnp.int32)[None, None, :]).astype(jnp.int32)
    before = jnp.cumsum(onehot, axis=1) - onehot
    position = jnp.sum(before * onehot, axis=2).astype(jnp.int32)
    block_ids = jnp.arange(blocks, dtype=jnp.int32)[:, None]
    target = (flattened * (blocks * CAP) + block_ids * CAP + position).reshape(-1).astype(jnp.int32)
    slot_total = EXPERTS * blocks * CAP
    tokens_twice = jnp.repeat(tokens, 2, axis=0)
    upstream_twice = jnp.repeat(upstream, 2, axis=0)
    gates_flat = route_gates.reshape(-1).astype(jnp.float32)
    buffer_x = jnp.zeros((slot_total, D), jnp.bfloat16).at[target].set(tokens_twice).reshape(EXPERTS, blocks * CAP, D)
    buffer_dy = jnp.zeros((slot_total, D), jnp.bfloat16).at[target].set(upstream_twice).reshape(EXPERTS, blocks * CAP, D)
    buffer_weight = jnp.zeros((slot_total,), jnp.float32).at[target].set(gates_flat).reshape(EXPERTS, blocks * CAP)
    grad_rows, gate_grad, grad_gate, grad_up, grad_down = lax.map(one_expert, (buffer_x, buffer_dy, buffer_weight, w_gate, w_up, w_down))
    row_grads = grad_rows.reshape(slot_total, D)[target]
    grad_tokens = jnp.sum(row_grads.reshape(TOKENS, 2, D), axis=1).astype(jnp.bfloat16)
    grad_gates = gate_grad.reshape(slot_total)[target].reshape(TOKENS, 2)
    return grad_tokens, grad_gates, grad_gate, grad_up, grad_down
```

```python
import jax
import jax.numpy as jnp
from jax import lax
from jax.sharding import PartitionSpec as P

PAD = 128


def contract_last(left, right):
    return lax.dot_general(
        left, right, (((1,), (1,)), ((), ())), preferred_element_type=jnp.float32
    )


def contract_first(left, right):
    return lax.dot_general(
        left, right, (((0,), (0,)), ((), ())), preferred_element_type=jnp.float32
    )


def swap(value, axis, mask):
    size = lax.axis_size(axis)
    return lax.ppermute(value, axis, [(i, i ^ mask) for i in range(size)])


def to_wire(total, features, experts):
    product = total[..., features : features + experts] + total[..., features + experts : features + 2 * experts]
    high = lax.reduce_precision(product, 8, 7)
    rest = jnp.zeros(total.shape[:-1] + (PAD - 2 * experts,), jnp.float32)
    return jnp.concatenate(
        [total[..., :features], high, product - high, rest], axis=-1
    ).astype(jnp.bfloat16)


def local(tokens, upstream, route_ids, route_gates, w_gate, w_up, w_down):
    experts = lax.axis_size("expert")
    groups = lax.axis_size("section") // 2
    tok_count, features = tokens.shape
    core = lax.axis_index("section") % 2
    own_expert = lax.axis_index("expert")
    first_core = core == 0

    chosen = route_ids[:, :, None] == jnp.arange(experts, dtype=jnp.int32)[None, None, :]
    dense = jnp.sum(jnp.where(chosen, route_gates[:, :, None].astype(jnp.float32), 0.0), axis=1)
    extra = jnp.pad(dense, ((0, 0), (0, PAD - experts))).astype(jnp.bfloat16)
    x_wide = jnp.concatenate([tokens, extra], axis=1)
    dy_wide = jnp.concatenate([upstream, extra], axis=1)

    got = swap(jnp.where(first_core, dy_wide, x_wide), "section", 1)
    kept = jnp.where(first_core, x_wide, dy_wide)
    block = jnp.concatenate(
        [jnp.where(first_core, kept, got), jnp.where(first_core, got, kept)], axis=0
    )
    along = [swap(block, "section", 2 * k) for k in range(1, groups)]
    near = [block] + [swap(block, "expert", d) for d in range(1, experts)]
    far_block = jnp.concatenate(along, axis=0)
    far = [far_block] + [swap(far_block, "expert", d) for d in range(1, experts)]
    pieces = [piece for pair in zip(near, far) for piece in pair]
    mine = jnp.concatenate(pieces, axis=0)
    other = jnp.concatenate([swap(piece, "section", 1) for piece in pieces], axis=0)
    rows_x = jnp.where(first_core, mine, other)
    rows_dy = jnp.where(first_core, other, mine)
    is_own = jnp.arange(experts, dtype=jnp.int32)[None, :] == own_expert
    weight = jnp.sum(
        jnp.where(is_own, rows_x[:, features : features + experts].astype(jnp.float32), 0.0),
        axis=1,
        keepdims=True,
    )
    rows_x = rows_x[:, :features]
    rows_dy = rows_dy[:, :features]

    gate_slab = w_gate[0]
    up_slab = w_up[0]
    down_slab = w_down[0]
    pre_gate = jnp.dot(rows_x, gate_slab, preferred_element_type=jnp.float32)
    pre_up = jnp.dot(rows_x, up_slab, preferred_element_type=jnp.float32)
    sigmoid_gate = jax.nn.sigmoid(pre_gate)
    active = pre_gate * sigmoid_gate
    hidden = (active * pre_up).astype(jnp.bfloat16)
    back_proj = contract_last(rows_dy, down_slab)
    d_hidden = weight * back_proj
    d_gate = (d_hidden * pre_up * (sigmoid_gate * (1.0 + pre_gate * (1.0 - sigmoid_gate)))).astype(
        jnp.bfloat16
    )
    d_up = (d_hidden * active).astype(jnp.bfloat16)
    scaled_up = (weight * rows_dy.astype(jnp.float32)).astype(jnp.bfloat16)
    product = jnp.sum(hidden.astype(jnp.float32) * back_proj, axis=1, keepdims=True)
    input_part = contract_last(d_gate, gate_slab) + contract_last(d_up, up_slab)
    grad_down = contract_first(hidden, scaled_up)
    grad_gate = contract_first(rows_x, d_gate)
    grad_up = contract_first(rows_x, d_up)

    spread = jnp.where(is_own, product, 0.0)
    wide = jnp.concatenate(
        [input_part, spread, jnp.zeros((spread.shape[0], PAD - experts), jnp.float32)], axis=1
    ).reshape(experts, groups, 2, tok_count, features + PAD)
    to_keep = jnp.where(first_core, wide[:, :, 0], wide[:, :, 1])
    to_send = jnp.where(first_core, wide[:, :, 1], wide[:, :, 0])
    total = [
        to_keep[d] + swap(to_wire(to_send[d], features, experts), "section", 1).astype(jnp.float32)
        for d in range(experts)
    ]
    plane = total[0]
    for d in range(1, experts):
        plane = plane + swap(to_wire(total[d], features, experts), "expert", d).astype(jnp.float32)
    final = plane[0]
    for k in range(1, groups):
        final = final + swap(to_wire(plane[k], features, experts), "section", 2 * k).astype(
            jnp.float32
        )
    grad_tokens = final[:, :features].astype(jnp.bfloat16)
    products = final[:, features : features + experts] + final[:, features + experts : features + 2 * experts]
    grad_gates = jnp.sum(jnp.where(chosen, products[:, None, :], 0.0), axis=2)
    return (
        grad_tokens,
        grad_gates,
        grad_gate.astype(jnp.bfloat16)[None],
        grad_up.astype(jnp.bfloat16)[None],
        grad_down.astype(jnp.bfloat16)[None],
    )


def solution(mesh):
    placed = (
        P(("section", "expert"), None),
        P(("section", "expert"), None),
        P(("section", "expert"), None),
        P(("section", "expert"), None),
        P("expert", None, "section"),
        P("expert", None, "section"),
        P("expert", "section", None),
    )
    return jax.shard_map(
        local,
        mesh=mesh,
        in_specs=placed,
        out_specs=(
            P(("section", "expert"), None),
            P(("section", "expert"), None),
            P("expert", None, "section"),
            P("expert", None, "section"),
            P("expert", "section", None),
        ),
        check_vma=False,
    )
```

```python
import functools

import jax
import jax.numpy as jnp
from jax import lax
from jax.experimental import pallas as pl
from jax.experimental.pallas import tpu as pltpu
from jax.sharding import PartitionSpec as P

PAD = 128
VMEM = 48 * 1024 * 1024
LARGEST = 256
BF = jnp.bfloat16
F32 = jnp.float32


def contract_last(left, right):
    return lax.dot_general(
        left, right, (((1,), (1,)), ((), ())), preferred_element_type=jnp.float32
    )


def contract_first(left, right):
    return lax.dot_general(
        left, right, (((0,), (0,)), ((), ())), preferred_element_type=jnp.float32
    )


def swap(value, axis, mask):
    size = lax.axis_size(axis)
    return lax.ppermute(value, axis, [(i, i ^ mask) for i in range(size)])


def call(body, outs, name, flops=0, moved=0):
    return pl.pallas_call(
        body,
        out_shape=outs,
        name=name,
        compiler_params=pltpu.CompilerParams(vmem_limit_bytes=VMEM),
        cost_estimate=pl.CostEstimate(flops=flops, bytes_accessed=moved, transcendentals=0),
    )


def shape(dims, dtype):
    return jax.ShapeDtypeStruct(dims, dtype)


def lanes(rows):
    return lax.broadcasted_iota(jnp.int32, (rows, PAD), 1)


def wire_pad(total, experts):
    lane = lanes(total.shape[0])
    rest = total - total.astype(BF).astype(F32)
    low = (lane >= experts) & (lane < 2 * experts)
    return jnp.where(low, total + pltpu.roll(rest, experts, 1), total).astype(BF)


def pack_body(x_ref, dy_ref, ids_ref, gates_ref, out_ref):
    count, features = x_ref.shape
    lane = lanes(count)
    gates = gates_ref[...].astype(F32)
    ids = ids_ref[...]
    dense = jnp.zeros((count, PAD), F32)
    for k in range(ids.shape[1]):
        dense = jnp.where(lane == ids[:, k : k + 1], gates[:, k : k + 1], dense)
    out_ref[:, :features] = jnp.concatenate(
        [x_ref[...].astype(F32), dy_ref[...].astype(F32)], axis=0
    ).astype(BF)
    out_ref[:, features:] = jnp.concatenate([dense, dense], axis=0).astype(BF)


def expert_body(experts, count, *refs):
    pieces, (wg_ref, wu_ref, wd_ref), rest = refs[:-12], refs[-12:-9], refs[-9:]
    x_ref, scaled_ref, hidden_ref, dg_ref, du_ref, send_ref, keep_ref, dy_ref, weight_ref = rest
    features = x_ref.shape[1]
    own = lax.axis_index("expert")
    lane = lanes(count)

    blocks = []
    for piece in pieces:
        for at in range(0, piece.shape[0], 2 * count):
            blocks.append((piece, at))
    for i in range(0, len(blocks), 2):
        halves = [ref[at : at + 2 * count, :].astype(F32) for ref, at in blocks[i : i + 2]]
        rows = pl.ds(i * count, 2 * count)
        x_ref[rows, :] = jnp.concatenate([h[:count, :features] for h in halves], axis=0).astype(BF)
        dy = jnp.concatenate([h[count:, :features] for h in halves], axis=0)
        dense = jnp.concatenate([h[:count, features:] for h in halves], axis=0)
        lane = lanes(2 * count)
        weight = jnp.sum(jnp.where(lane == own, dense, 0.0), axis=1, keepdims=True)
        weight_ref[rows, :] = jnp.broadcast_to(weight, (2 * count, PAD))
        dy_ref[rows, :] = dy.astype(BF)
        scaled_ref[rows, :] = (weight * dy).astype(BF)

    pre_gate = jnp.dot(x_ref[...], wg_ref[0], preferred_element_type=F32)
    pre_up = jnp.dot(x_ref[...], wu_ref[0], preferred_element_type=F32)
    back = contract_last(dy_ref[...], wd_ref[0])
    sig = jax.nn.sigmoid(pre_gate)
    active = pre_gate * sig
    hidden = (active * pre_up).astype(BF)
    d_hidden = weight_ref[:, :1] * back
    d_gate = (d_hidden * pre_up * (sig * (1.0 + pre_gate * (1.0 - sig)))).astype(BF)
    d_up = (d_hidden * active).astype(BF)
    hidden_ref[...] = hidden
    dg_ref[...] = d_gate
    du_ref[...] = d_up
    product = jnp.sum(hidden.astype(F32) * back, axis=1, keepdims=True)
    half = product.shape[0] // 2
    spread = jnp.where(lanes(2 * half) == own, product, 0.0)
    part = contract_last(d_gate[half:], wg_ref[0]) + contract_last(d_up[half:], wu_ref[0])
    send_ref[:, :features] = part.astype(BF)
    send_ref[:, features:] = wire_pad(spread[half:], experts)
    keep_ref[:, :features] = contract_last(d_gate[:half], wg_ref[0]) + contract_last(
        d_up[:half], wu_ref[0]
    )
    keep_ref[:, features:] = spread[:half]


def sum_body(experts, added, *refs):
    keep_ref, parts, outs = refs[0], refs[1 : 1 + added], refs[1 + added :]
    rows, width = outs[0].shape
    for i, out in enumerate(outs):
        at = pl.ds(i * rows, rows)
        total = keep_ref[at, :]
        for part in parts:
            total = total + part[at, :].astype(F32)
        if i == 0:
            out[...] = total
        else:
            out[:, : width - PAD] = total[:, : width - PAD].astype(BF)
            out[:, width - PAD :] = wire_pad(total[:, width - PAD :], experts)


def sum_parts(keep, parts, pieces, experts, name):
    rows = keep.shape[0] // pieces
    dims = (rows, keep.shape[1])
    outs = [shape(dims, F32)] + [shape(dims, BF)] * (pieces - 1)
    moved = 2 * keep.size * (2 + len(parts))
    return call(
        functools.partial(sum_body, experts, len(parts)), outs, name, keep.size * len(parts), moved
    )(keep, *parts)


def final_body(experts, added, *refs):
    keep_ref, parts, (ids_ref, tokens_ref, gates_ref) = refs[0], refs[1 : 1 + added], refs[1 + added :]
    count, features = tokens_ref.shape
    total = keep_ref[...]
    for part in parts:
        total = total + part[...].astype(F32)
    tokens_ref[...] = total[:, :features].astype(BF)
    ids = ids_ref[...]
    product = total[:, features:]
    lane = lanes(count)
    for k in range(ids.shape[1]):
        id_k = ids[:, k : k + 1]
        picked = (lane == id_k) | (lane == id_k + experts)
        gates_ref[:, k : k + 1] = jnp.sum(jnp.where(picked, product, 0.0), axis=1, keepdims=True)


def expert_plain(pieces, slabs, experts, count):
    gate_slab, up_slab, down_slab = slabs
    features = gate_slab.shape[0]
    rows = jnp.concatenate(pieces, axis=0).reshape(-1, 2, count, features + PAD)
    rows_x = rows[:, 0].reshape(-1, features + PAD)
    rows_dy = rows[:, 1, :, :features].reshape(-1, features)
    is_own = jnp.arange(PAD, dtype=jnp.int32)[None, :] == lax.axis_index("expert")
    weight = jnp.sum(
        jnp.where(is_own, rows_x[:, features:].astype(F32), 0.0), axis=1, keepdims=True
    )
    rows_x = rows_x[:, :features]
    pre_gate = jnp.dot(rows_x, gate_slab, preferred_element_type=F32)
    pre_up = jnp.dot(rows_x, up_slab, preferred_element_type=F32)
    back = contract_last(rows_dy, down_slab)
    sig = jax.nn.sigmoid(pre_gate)
    active = pre_gate * sig
    hidden = (active * pre_up).astype(BF)
    d_hidden = weight * back
    d_gate = (d_hidden * pre_up * (sig * (1.0 + pre_gate * (1.0 - sig)))).astype(BF)
    d_up = (d_hidden * active).astype(BF)
    scaled = (weight * rows_dy.astype(F32)).astype(BF)
    product = jnp.sum(hidden.astype(F32) * back, axis=1, keepdims=True)
    half = product.shape[0] // 2
    part = contract_last(d_gate, gate_slab) + contract_last(d_up, up_slab)
    wide = jnp.concatenate([part, jnp.where(is_own, product, 0.0)], axis=1)
    send = to_wire(wide[half:], experts)
    return rows_x, scaled, hidden, d_gate, d_up, send, wide[:half]


def to_wire(total, experts):
    pad = total[:, -PAD:]
    rest = jnp.roll(pad - lax.reduce_precision(pad, 8, 7), experts, 1)
    lane = jnp.arange(PAD)[None, :]
    pad = jnp.where((lane >= experts) & (lane < 2 * experts), pad + rest, pad)
    return jnp.concatenate([total[:, :-PAD], pad], axis=1).astype(BF)


def sum_plain(keep, parts, pieces, experts):
    for part in parts:
        keep = keep + part.astype(F32)
    split = jnp.split(keep, pieces, axis=0)
    return split[:1] + [to_wire(piece, experts) for piece in split[1:]]


def local(tokens, upstream, route_ids, route_gates, w_gate, w_up, w_down):
    experts = lax.axis_size("expert")
    groups = lax.axis_size("section") // 2
    count, features = tokens.shape
    width = features + PAD
    total_rows = 2 * experts * groups * count
    hidden_units = w_gate.shape[2]

    block = call(pack_body, shape((2 * count, width), BF), "pack", 0, 4 * count * width * 2)(
        tokens, upstream, route_ids, route_gates
    )
    along = [swap(block, "section", 2 * k) for k in range(1, groups)]
    near = [block] + [swap(block, "expert", d) for d in range(1, experts)]
    far_block = jnp.concatenate(along, axis=0)
    far = [far_block] + [swap(far_block, "expert", d) for d in range(1, experts)]
    mine = [piece for pair in zip(near, far) for piece in pair]
    pieces = mine + [swap(piece, "section", 1) for piece in mine]

    fits = total_rows <= LARGEST
    if fits:
        rows_x, scaled, hidden, d_gate, d_up, send, keep = pl.pallas_call(
            functools.partial(expert_body, experts, count),
            out_shape=[
                shape((total_rows, features), BF),
                shape((total_rows, features), BF),
                shape((total_rows, hidden_units), BF),
                shape((total_rows, hidden_units), BF),
                shape((total_rows, hidden_units), BF),
                shape((total_rows // 2, width), BF),
                shape((total_rows // 2, width), F32),
            ],
            scratch_shapes=[
                pltpu.VMEM((total_rows, features), BF),
                pltpu.VMEM((total_rows, PAD), F32),
            ],
            name="expert",
            compiler_params=pltpu.CompilerParams(vmem_limit_bytes=VMEM),
            cost_estimate=pl.CostEstimate(
                flops=10 * total_rows * features * hidden_units,
                bytes_accessed=16 * 1024 * 1024,
                transcendentals=total_rows * hidden_units,
            ),
        )(*pieces, w_gate, w_up, w_down)
    else:
        rows_x, scaled, hidden, d_gate, d_up, send, keep = expert_plain(
            pieces, (w_gate[0], w_up[0], w_down[0]), experts, count
        )

    def added(total, parts, pieces, name):
        if fits:
            return sum_parts(total, parts, pieces, experts, name)
        return sum_plain(total, parts, pieces, experts)

    split = added(keep, [swap(send, "section", 1)], experts, "sum_cores")
    plane = added(
        split[0], [swap(split[d], "expert", d) for d in range(1, experts)], groups, "sum_experts"
    )
    parts = [swap(plane[k], "section", 2 * k) for k in range(1, groups)]
    grad_tokens, grad_gates = call(
        functools.partial(final_body, experts, len(parts)),
        [shape((count, features), BF), shape(route_ids.shape, F32)],
        "final",
        0,
        4 * count * width * 2,
    )(plane[0], *parts, route_ids)

    grad_down = contract_first(hidden, scaled)
    grad_gate = contract_first(rows_x, d_gate)
    grad_up = contract_first(rows_x, d_up)
    return (
        grad_tokens,
        grad_gates,
        grad_gate.astype(BF)[None],
        grad_up.astype(BF)[None],
        grad_down.astype(BF)[None],
    )


def solution(mesh):
    placed = (
        P(("section", "expert"), None),
        P(("section", "expert"), None),
        P(("section", "expert"), None),
        P(("section", "expert"), None),
        P("expert", None, "section"),
        P("expert", None, "section"),
        P("expert", "section", None),
    )
    return jax.shard_map(
        local,
        mesh=mesh,
        in_specs=placed,
        out_specs=(
            P(("section", "expert"), None),
            P(("section", "expert"), None),
            P("expert", None, "section"),
            P("expert", None, "section"),
            P("expert", "section", None),
        ),
        check_vma=False,
    )
```

```python
import functools

import jax
import jax.numpy as jnp
from jax import lax
from jax.experimental import pallas as pl
from jax.experimental.pallas import tpu as pltpu
from jax.sharding import PartitionSpec as P

PAD = 128
MIB = 1024 * 1024
VMEM = 24 * MIB
LARGEST = 256
BF = jnp.bfloat16
F32 = jnp.float32


def contract_last(left, right):
    return lax.dot_general(
        left, right, (((1,), (1,)), ((), ())), preferred_element_type=jnp.float32
    )


def contract_first(left, right):
    return lax.dot_general(
        left, right, (((0,), (0,)), ((), ())), preferred_element_type=jnp.float32
    )


def swap(value, axis, mask):
    size = lax.axis_size(axis)
    return lax.ppermute(value, axis, [(i, i ^ mask) for i in range(size)])


def call(body, outs, name, flops=0, moved=0):
    return pl.pallas_call(
        body,
        out_shape=outs,
        name=name,
        compiler_params=pltpu.CompilerParams(vmem_limit_bytes=VMEM),
        cost_estimate=pl.CostEstimate(flops=flops, bytes_accessed=moved, transcendentals=0),
    )


def shape(dims, dtype):
    return jax.ShapeDtypeStruct(dims, dtype)


def lanes(rows):
    return lax.broadcasted_iota(jnp.int32, (rows, PAD), 1)


def wire_pad(total, experts):
    lane = lanes(total.shape[0])
    rest = total - total.astype(BF).astype(F32)
    low = (lane >= experts) & (lane < 2 * experts)
    return jnp.where(low, total + pltpu.roll(rest, experts, 1), total).astype(BF)


def column(row):
    count = row.shape[1]
    here = lax.broadcasted_iota(jnp.int32, (count, count), 0)
    there = lax.broadcasted_iota(jnp.int32, (count, count), 1)
    return jnp.sum(jnp.where(here == there, row, 0.0), axis=1, keepdims=True)


def as_row(col):
    count = col.shape[0]
    here = lax.broadcasted_iota(jnp.int32, (count, count), 0)
    there = lax.broadcasted_iota(jnp.int32, (count, count), 1)
    return jnp.sum(jnp.where(here == there, col, 0.0), axis=0, keepdims=True)


def pack_body(x_hbm, dy_hbm, ids_hbm, gates_hbm, out_ref, x_ref, dy_ref, ids_ref, gates_ref, sems):
    pairs = ((ids_hbm, ids_ref), (gates_hbm, gates_ref), (x_hbm, x_ref), (dy_hbm, dy_ref))
    copies = [pltpu.make_async_copy(src, dst, sems.at[i]) for i, (src, dst) in enumerate(pairs)]
    for copy in copies:
        copy.start()
    for copy in copies:
        copy.wait()
    count, features = x_ref.shape
    lane = lanes(count).astype(F32)
    gates = gates_ref[...].astype(F32)
    ids = ids_ref[...].astype(F32)
    dense = jnp.zeros((count, PAD), F32)
    for k in range(ids.shape[0]):
        dense = jnp.where(lane == column(ids[k : k + 1]), column(gates[k : k + 1]), dense)
    out_ref[:, :features] = jnp.concatenate(
        [x_ref[...].astype(F32), dy_ref[...].astype(F32)], axis=0
    ).astype(BF)
    out_ref[:, features:] = jnp.concatenate([dense, dense], axis=0).astype(BF)


def expert_body(experts, count, load, pieces_count, *refs):
    pieces, given, rest = refs[:pieces_count], refs[pieces_count : pieces_count + 3], refs[pieces_count + 3 :]
    x_ref, scaled_ref, hidden_ref, dg_ref, du_ref, send_ref, keep_ref = rest[:7]
    copies = []
    if load:
        wg_ref, wu_ref, wd_ref, dy_ref, weight_ref, sems = rest[7:]
        for i, (src, dst) in enumerate(zip(given, (wg_ref, wu_ref, wd_ref))):
            copies.append(pltpu.make_async_copy(src, dst, sems.at[i]))
            copies[i].start()
    else:
        wg_ref, wu_ref, wd_ref = given
        dy_ref, weight_ref = rest[7:]
    features = x_ref.shape[1]
    own = lax.axis_index("expert")
    lane = lanes(count)

    blocks = []
    for piece in pieces:
        for at in range(0, piece.shape[0], 2 * count):
            blocks.append((piece, at))
    for i in range(0, len(blocks), 2):
        halves = [ref[at : at + 2 * count, :].astype(F32) for ref, at in blocks[i : i + 2]]
        rows = pl.ds(i * count, 2 * count)
        x_ref[rows, :] = jnp.concatenate([h[:count, :features] for h in halves], axis=0).astype(BF)
        dy = jnp.concatenate([h[count:, :features] for h in halves], axis=0)
        dense = jnp.concatenate([h[:count, features:] for h in halves], axis=0)
        lane = lanes(2 * count)
        weight = jnp.sum(jnp.where(lane == own, dense, 0.0), axis=1, keepdims=True)
        weight_ref[rows, :] = jnp.broadcast_to(weight, (2 * count, PAD))
        dy_ref[rows, :] = dy.astype(BF)
        scaled_ref[rows, :] = (weight * dy).astype(BF)

    if load:
        copies[0].wait()
    pre_gate = jnp.dot(x_ref[...], wg_ref[0], preferred_element_type=F32)
    if load:
        copies[1].wait()
    pre_up = jnp.dot(x_ref[...], wu_ref[0], preferred_element_type=F32)
    if load:
        copies[2].wait()
    back = contract_last(dy_ref[...], wd_ref[0])
    sig = jax.nn.sigmoid(pre_gate)
    active = pre_gate * sig
    hidden = (active * pre_up).astype(BF)
    d_hidden = weight_ref[:, :1] * back
    d_gate = (d_hidden * pre_up * (sig * (1.0 + pre_gate * (1.0 - sig)))).astype(BF)
    d_up = (d_hidden * active).astype(BF)
    hidden_ref[...] = hidden
    dg_ref[...] = d_gate
    du_ref[...] = d_up
    product = jnp.sum(hidden.astype(F32) * back, axis=1, keepdims=True)
    half = product.shape[0] // 2
    spread = jnp.where(lanes(2 * half) == own, product, 0.0)
    part = contract_last(d_gate[half:], wg_ref[0]) + contract_last(d_up[half:], wu_ref[0])
    send_ref[:, :features] = part.astype(BF)
    send_ref[:, features:] = wire_pad(spread[half:], experts)
    keep_ref[:, :features] = contract_last(d_gate[:half], wg_ref[0]) + contract_last(
        d_up[:half], wu_ref[0]
    )
    keep_ref[:, features:] = spread[:half]


def sum_body(experts, added, stays, *refs):
    keep_ref, parts, outs = refs[0], refs[1 : 1 + added], refs[1 + added :]
    rows, width = outs[0].shape
    for i, out in enumerate(outs):
        at = pl.ds(i * rows, rows)
        total = keep_ref[at, :]
        for part in parts:
            total = total + part[at, :].astype(F32)
        if i == 0 and stays:
            out[...] = total
        else:
            out[:, : width - PAD] = total[:, : width - PAD].astype(BF)
            out[:, width - PAD :] = wire_pad(total[:, width - PAD :], experts)


def sum_parts(keep, parts, pieces, stays, experts, name):
    rows = keep.shape[0] // pieces
    dims = (rows, keep.shape[1])
    outs = [shape(dims, F32 if stays and i == 0 else BF) for i in range(pieces)]
    moved = 2 * keep.size * (2 + len(parts))
    return call(
        functools.partial(sum_body, experts, len(parts), stays),
        outs,
        name,
        keep.size * len(parts),
        moved,
    )(keep, *parts)


def join_body(experts, count, where, keep_a, keep_b, send_a, send_b, *refs):
    outs, total_ref = refs[:-1], refs[-1]
    rows = keep_a.shape[0]
    total_ref[:rows, :] = keep_a[...] + send_a[...].astype(F32)
    total_ref[rows:, :] = keep_b[...] + send_b[...].astype(F32)
    features = total_ref.shape[1] - PAD
    for d, places in enumerate(where):
        total = jnp.concatenate(
            [total_ref[i * count : (i + 1) * count, :] for i in places], axis=0
        )
        if d == 0:
            outs[d][...] = total
        else:
            outs[d][:, :features] = total[:, :features].astype(BF)
            outs[d][:, features:] = wire_pad(total[:, features:], experts)


def final_body(experts, added, *refs):
    keep_ref, parts, (ids_ref, tokens_ref, gates_ref) = refs[0], refs[1 : 1 + added], refs[1 + added :]
    count, features = tokens_ref.shape
    total = keep_ref[...]
    for part in parts:
        total = total + part[...].astype(F32)
    tokens_ref[...] = total[:, :features].astype(BF)
    product = total[:, features:]
    lane = lanes(count).astype(F32)
    ids = ids_ref[...].astype(F32)
    for k in range(ids.shape[0]):
        id_k = column(ids[k : k + 1])
        picked = (lane == id_k) | (lane == id_k + experts)
        gates_ref[k : k + 1, :] = as_row(
            jnp.sum(jnp.where(picked, product, 0.0), axis=1, keepdims=True)
        )


def expert_plain(pieces, slabs, experts, count):
    gate_slab, up_slab, down_slab = slabs
    features = gate_slab.shape[0]
    rows = jnp.concatenate(pieces, axis=0).reshape(-1, 2, count, features + PAD)
    rows_x = rows[:, 0].reshape(-1, features + PAD)
    rows_dy = rows[:, 1, :, :features].reshape(-1, features)
    is_own = jnp.arange(PAD, dtype=jnp.int32)[None, :] == lax.axis_index("expert")
    weight = jnp.sum(
        jnp.where(is_own, rows_x[:, features:].astype(F32), 0.0), axis=1, keepdims=True
    )
    rows_x = rows_x[:, :features]
    pre_gate = jnp.dot(rows_x, gate_slab, preferred_element_type=F32)
    pre_up = jnp.dot(rows_x, up_slab, preferred_element_type=F32)
    back = contract_last(rows_dy, down_slab)
    sig = jax.nn.sigmoid(pre_gate)
    active = pre_gate * sig
    hidden = (active * pre_up).astype(BF)
    d_hidden = weight * back
    d_gate = (d_hidden * pre_up * (sig * (1.0 + pre_gate * (1.0 - sig)))).astype(BF)
    d_up = (d_hidden * active).astype(BF)
    scaled = (weight * rows_dy.astype(F32)).astype(BF)
    product = jnp.sum(hidden.astype(F32) * back, axis=1, keepdims=True)
    half = product.shape[0] // 2
    part = contract_last(d_gate, gate_slab) + contract_last(d_up, up_slab)
    wide = jnp.concatenate([part, jnp.where(is_own, product, 0.0)], axis=1)
    send = to_wire(wide[half:], experts)
    return rows_x, scaled, hidden, d_gate, d_up, send, wide[:half]


def to_wire(total, experts):
    pad = total[:, -PAD:]
    rest = jnp.roll(pad - lax.reduce_precision(pad, 8, 7), experts, 1)
    lane = jnp.arange(PAD)[None, :]
    pad = jnp.where((lane >= experts) & (lane < 2 * experts), pad + rest, pad)
    return jnp.concatenate([total[:, :-PAD], pad], axis=1).astype(BF)


def sum_plain(keep, parts, pieces, stays, experts):
    for part in parts:
        keep = keep + part.astype(F32)
    split = jnp.split(keep, pieces, axis=0)
    return [
        piece if stays and i == 0 else to_wire(piece, experts) for i, piece in enumerate(split)
    ]


def expert_step(pieces, weights, experts, count, limit, load):
    w_gate, w_up, w_down = weights
    rows = sum(piece.shape[0] for piece in pieces) // 2
    features, hidden_units = w_gate.shape[1:]
    width = features + PAD
    if rows > limit:
        return *expert_plain(pieces, (w_gate[0], w_up[0], w_down[0]), experts, count), *weights
    outs = [
        shape((rows, features), BF),
        shape((rows, features), BF),
        shape((rows, hidden_units), BF),
        shape((rows, hidden_units), BF),
        shape((rows, hidden_units), BF),
        shape((rows // 2, width), BF),
        shape((rows // 2, width), F32),
    ]
    scratch = [pltpu.VMEM((rows, features), BF), pltpu.VMEM((rows, PAD), F32)]
    weight_space = pltpu.VMEM
    if load:
        outs += [shape(w.shape, BF) for w in weights]
        scratch.append(pltpu.SemaphoreType.DMA((3,)))
        weight_space = pltpu.HBM
    specs = [pl.BlockSpec(memory_space=pltpu.VMEM)] * len(pieces)
    result = pl.pallas_call(
        functools.partial(expert_body, experts, count, load, len(pieces)),
        out_shape=outs,
        in_specs=specs + [pl.BlockSpec(memory_space=weight_space)] * 3,
        scratch_shapes=scratch,
        name="expert",
        compiler_params=pltpu.CompilerParams(vmem_limit_bytes=(44 if load else 24) * MIB),
        cost_estimate=pl.CostEstimate(
            flops=0,
            bytes_accessed=1024,
            transcendentals=0,
        ),
    )(*pieces, *weights)
    return result if load else [*result, *weights]


def local(tokens, upstream, route_ids, route_gates, w_gate, w_up, w_down):
    experts = lax.axis_size("expert")
    groups = lax.axis_size("section") // 2
    count, features = tokens.shape
    width = features + PAD
    fits = 2 * experts * groups * count <= LARGEST
    ids, gates = route_ids.T, route_gates.T

    block = pl.pallas_call(
        pack_body,
        out_shape=shape((2 * count, width), BF),
        in_specs=[pl.BlockSpec(memory_space=pltpu.HBM)] * 4,
        scratch_shapes=[
            pltpu.VMEM(tokens.shape, BF),
            pltpu.VMEM(tokens.shape, BF),
            pltpu.VMEM(ids.shape, jnp.int32),
            pltpu.VMEM(ids.shape, BF),
            pltpu.SemaphoreType.DMA((4,)),
        ],
        name="pack",
        compiler_params=pltpu.CompilerParams(vmem_limit_bytes=60 * MIB),
    )(tokens, upstream, ids, gates)

    def to_others(value):
        return [value] + [swap(value, "expert", d) for d in range(1, experts)]

    def added(total, parts, pieces, stays, name):
        if fits:
            return sum_parts(total, parts, pieces, stays, experts, name)
        return sum_plain(total, parts, pieces, stays, experts)

    along = [swap(block, "section", 2 * k) for k in range(groups - 1, 0, -1)][::-1]
    others = sorted(range(1, experts), key=lambda d: -d.bit_count())
    near = {0: block}
    for d in range(1, experts):
        near[d] = swap(near[d & (d - 1)], "expert", d & -d)
    early = [d for d in range(1, experts) if d.bit_count() == 1]
    late = [d for d in others if d not in early]
    far_block = jnp.concatenate(along[1:], axis=0)
    near_block = jnp.concatenate([near[d] for d in others], axis=0)
    held = [along[0]] + [near[d] for d in early]
    far_block, near_block, held = lax.optimization_barrier((far_block, near_block, held))
    far = [swap(far_block, "expert", d) for d in others] + [swap(near_block, "section", 2)]

    limit = LARGEST if fits else 0
    order = [(0, k) for k in range(groups)] + [(d, 0) for d in early]
    mine = jnp.concatenate([block, held[0], far_block] + held[1:], axis=0)
    *first, w_gate, w_up, w_down = expert_step(
        [mine, swap(mine, "section", 1)], (w_gate, w_up, w_down), experts, count, limit, True
    )
    order += [(d, 0) for d in late] + [(d, k) for d in others for k in range(2, groups)]
    order += [(d, 1) for d in others]
    mine = [near[d] for d in late] + far
    mine, first[5] = lax.optimization_barrier((mine, first[5]))
    second = expert_step(
        mine + [swap(piece, "section", 1) for piece in mine],
        (w_gate, w_up, w_down),
        experts,
        count,
        limit,
        False,
    )[:7]
    steps = [first, second]
    sends = [swap(step[5], "section", 1) for step in steps]
    keeps = [step[6] for step in steps]
    where = [[order.index((d, k)) for k in range(groups)] for d in range(experts)]
    if fits:
        dims = (groups * count, width)
        split = pl.pallas_call(
            functools.partial(join_body, experts, count, where),
            out_shape=[shape(dims, BF if d else F32) for d in range(experts)],
            scratch_shapes=[pltpu.VMEM((experts * groups * count, width), F32)],
            name="sum_cores",
            compiler_params=pltpu.CompilerParams(vmem_limit_bytes=VMEM),
            cost_estimate=pl.CostEstimate(flops=0, bytes_accessed=1024, transcendentals=0),
        )(*keeps, *sends)
    else:
        total = jnp.concatenate(keeps, axis=0) + jnp.concatenate(sends, axis=0).astype(F32)
        blocks = total.reshape(-1, count, width)
        split = [jnp.concatenate([blocks[i] for i in places], axis=0) for places in where]
        split = [to_wire(part, experts) if d else part for d, part in enumerate(split)]
    arrived = [swap(part, "expert", d) if d else part for d, part in enumerate(split)]
    plane = added(arrived[0], arrived[1:], groups, True, "sum_experts")
    kept = plane[0]
    parts = [swap(plane[k], "section", 2 * k) for k in range(1, groups)]
    grad_tokens, grad_gates = call(
        functools.partial(final_body, experts, len(parts)),
        [shape((count, features), BF), shape(ids.shape, F32)],
        "final",
        0,
        4 * count * width * 2,
    )(kept, *parts, ids)

    rows_x, scaled, hidden, d_gate, d_up = [
        jnp.concatenate(both, axis=0) for both in list(zip(*steps))[:5]
    ]
    grad_down = contract_first(hidden, scaled)
    grad_gate = contract_first(rows_x, d_gate)
    grad_up = contract_first(rows_x, d_up)
    return (
        grad_tokens,
        grad_gates.T,
        grad_gate.astype(BF)[None],
        grad_up.astype(BF)[None],
        grad_down.astype(BF)[None],
    )


def solution(mesh):
    placed = (
        P(("section", "expert"), None),
        P(("section", "expert"), None),
        P(("section", "expert"), None),
        P(("section", "expert"), None),
        P("expert", None, "section"),
        P("expert", None, "section"),
        P("expert", "section", None),
    )
    return jax.shard_map(
        local,
        mesh=mesh,
        in_specs=placed,
        out_specs=(
            P(("section", "expert"), None),
            P(("section", "expert"), None),
            P("expert", None, "section"),
            P("expert", None, "section"),
            P("expert", "section", None),
        ),
        check_vma=False,
    )
```

```python
import functools

import jax
import jax.numpy as jnp
from jax import lax
from jax.experimental import pallas as pl
from jax.experimental.pallas import tpu as pltpu
from jax.sharding import PartitionSpec as P

PAD = 128
MIB = 1024 * 1024
VMEM = 24 * MIB
LARGEST = 256
BF = jnp.bfloat16
F32 = jnp.float32


def contract_last(left, right):
    return lax.dot_general(
        left, right, (((1,), (1,)), ((), ())), preferred_element_type=jnp.float32
    )


def contract_first(left, right):
    return lax.dot_general(
        left, right, (((0,), (0,)), ((), ())), preferred_element_type=jnp.float32
    )


def swap(value, axis, mask):
    size = lax.axis_size(axis)
    return lax.ppermute(value, axis, [(i, i ^ mask) for i in range(size)])


def call(body, outs, name, flops=0, moved=0):
    return pl.pallas_call(
        body,
        out_shape=outs,
        name=name,
        compiler_params=pltpu.CompilerParams(vmem_limit_bytes=VMEM),
        cost_estimate=pl.CostEstimate(flops=flops, bytes_accessed=moved, transcendentals=0),
    )


def shape(dims, dtype):
    return jax.ShapeDtypeStruct(dims, dtype)


def lanes(rows):
    return lax.broadcasted_iota(jnp.int32, (rows, PAD), 1)


def wire_pad(total, experts):
    lane = lanes(total.shape[0])
    rest = total - total.astype(BF).astype(F32)
    low = (lane >= experts) & (lane < 2 * experts)
    return jnp.where(low, total + pltpu.roll(rest, experts, 1), total).astype(BF)


def column(row):
    count = row.shape[1]
    here = lax.broadcasted_iota(jnp.int32, (count, count), 0)
    there = lax.broadcasted_iota(jnp.int32, (count, count), 1)
    return jnp.sum(jnp.where(here == there, row, 0.0), axis=1, keepdims=True)


def as_row(col):
    count = col.shape[0]
    here = lax.broadcasted_iota(jnp.int32, (count, count), 0)
    there = lax.broadcasted_iota(jnp.int32, (count, count), 1)
    return jnp.sum(jnp.where(here == there, col, 0.0), axis=0, keepdims=True)


def pack_body(x_hbm, dy_hbm, ids_hbm, gates_hbm, out_ref, x_ref, dy_ref, ids_ref, gates_ref, sems):
    pairs = ((ids_hbm, ids_ref), (gates_hbm, gates_ref), (x_hbm, x_ref), (dy_hbm, dy_ref))
    copies = [pltpu.make_async_copy(src, dst, sems.at[i]) for i, (src, dst) in enumerate(pairs)]
    for copy in copies:
        copy.start()
    for copy in copies:
        copy.wait()
    count, features = x_ref.shape
    lane = lanes(count).astype(F32)
    gates = gates_ref[...].astype(F32)
    ids = ids_ref[...].astype(F32)
    dense = jnp.zeros((count, PAD), F32)
    for k in range(ids.shape[0]):
        dense = jnp.where(lane == column(ids[k : k + 1]), column(gates[k : k + 1]), dense)
    out_ref[:, :features] = jnp.concatenate(
        [x_ref[...].astype(F32), dy_ref[...].astype(F32)], axis=0
    ).astype(BF)
    out_ref[:, features:] = jnp.concatenate([dense, dense], axis=0).astype(BF)


def expert_body(experts, count, load, pieces_count, *refs):
    pieces, given, rest = refs[:pieces_count], refs[pieces_count : pieces_count + 3], refs[pieces_count + 3 :]
    x_ref, scaled_ref, hidden_ref, dg_ref, du_ref, send_ref, keep_ref = rest[:7]
    copies = []
    if load:
        wg_ref, wu_ref, wd_ref, dy_ref, weight_ref, sems = rest[7:]
        for i, (src, dst) in enumerate(zip(given, (wg_ref, wu_ref, wd_ref))):
            copies.append(pltpu.make_async_copy(src, dst, sems.at[i]))
            copies[i].start()
    else:
        wg_ref, wu_ref, wd_ref = given
        dy_ref, weight_ref = rest[7:]
    features = x_ref.shape[1]
    own = lax.axis_index("expert")
    lane = lanes(count)

    blocks = []
    for piece in pieces:
        for at in range(0, piece.shape[0], 2 * count):
            blocks.append((piece, at))
    for i in range(0, len(blocks), 2):
        halves = [ref[at : at + 2 * count, :].astype(F32) for ref, at in blocks[i : i + 2]]
        rows = pl.ds(i * count, 2 * count)
        x_ref[rows, :] = jnp.concatenate([h[:count, :features] for h in halves], axis=0).astype(BF)
        dy = jnp.concatenate([h[count:, :features] for h in halves], axis=0)
        dense = jnp.concatenate([h[:count, features:] for h in halves], axis=0)
        lane = lanes(2 * count)
        weight = jnp.sum(jnp.where(lane == own, dense, 0.0), axis=1, keepdims=True)
        weight_ref[rows, :] = jnp.broadcast_to(weight, (2 * count, PAD))
        dy_ref[rows, :] = dy.astype(BF)
        scaled_ref[rows, :] = (weight * dy).astype(BF)

    if load:
        copies[0].wait()
    pre_gate = jnp.dot(x_ref[...], wg_ref[0], preferred_element_type=F32)
    if load:
        copies[1].wait()
    pre_up = jnp.dot(x_ref[...], wu_ref[0], preferred_element_type=F32)
    if load:
        copies[2].wait()
    back = contract_last(dy_ref[...], wd_ref[0])
    sig = jax.nn.sigmoid(pre_gate)
    active = pre_gate * sig
    hidden = (active * pre_up).astype(BF)
    d_hidden = weight_ref[:, :1] * back
    d_gate = (d_hidden * pre_up * (sig * (1.0 + pre_gate * (1.0 - sig)))).astype(BF)
    d_up = (d_hidden * active).astype(BF)
    hidden_ref[...] = hidden
    dg_ref[...] = d_gate
    du_ref[...] = d_up
    product = jnp.sum(hidden.astype(F32) * back, axis=1, keepdims=True)
    half = product.shape[0] // 2
    spread = jnp.where(lanes(2 * half) == own, product, 0.0)
    part = contract_last(d_gate[half:], wg_ref[0]) + contract_last(d_up[half:], wu_ref[0])
    send_ref[:, :features] = part.astype(BF)
    send_ref[:, features:] = wire_pad(spread[half:], experts)
    keep_ref[:, :features] = contract_last(d_gate[:half], wg_ref[0]) + contract_last(
        d_up[:half], wu_ref[0]
    )
    keep_ref[:, features:] = spread[:half]


def sum_body(experts, added, stays, *refs):
    keep_ref, parts, outs = refs[0], refs[1 : 1 + added], refs[1 + added :]
    rows, width = outs[0].shape
    for i, out in enumerate(outs):
        at = pl.ds(i * rows, rows)
        total = keep_ref[at, :]
        for part in parts:
            total = total + part[at, :].astype(F32)
        if i == 0 and stays:
            out[...] = total
        else:
            out[:, : width - PAD] = total[:, : width - PAD].astype(BF)
            out[:, width - PAD :] = wire_pad(total[:, width - PAD :], experts)


def sum_parts(keep, parts, pieces, stays, experts, name):
    rows = keep.shape[0] // pieces
    dims = (rows, keep.shape[1])
    outs = [shape(dims, F32 if stays and i == 0 else BF) for i in range(pieces)]
    moved = 2 * keep.size * (2 + len(parts))
    return call(
        functools.partial(sum_body, experts, len(parts), stays),
        outs,
        name,
        keep.size * len(parts),
        moved,
    )(keep, *parts)


def join_body(experts, count, where, keep_a, keep_b, send_a, send_b, *refs):
    outs, total_ref = refs[:-1], refs[-1]
    rows = keep_a.shape[0]
    total_ref[:rows, :] = keep_a[...] + send_a[...].astype(F32)
    total_ref[rows:, :] = keep_b[...] + send_b[...].astype(F32)
    features = total_ref.shape[1] - PAD
    for i, places in enumerate(where):
        total = jnp.concatenate(
            [total_ref[i * count : (i + 1) * count, :] for i in places], axis=0
        )
        if i < 2:
            outs[i][...] = total
        else:
            outs[i][:, :features] = total[:, :features].astype(BF)
            outs[i][:, features:] = wire_pad(total[:, features:], experts)


def final_body(experts, added, *refs):
    keep_ref, parts, (ids_ref, tokens_ref, gates_ref) = refs[0], refs[1 : 1 + added], refs[1 + added :]
    count, features = tokens_ref.shape
    total = keep_ref[...]
    for part in parts:
        total = total + part[...].astype(F32)
    tokens_ref[...] = total[:, :features].astype(BF)
    product = total[:, features:]
    lane = lanes(count).astype(F32)
    ids = ids_ref[...].astype(F32)
    for k in range(ids.shape[0]):
        id_k = column(ids[k : k + 1])
        picked = (lane == id_k) | (lane == id_k + experts)
        gates_ref[k : k + 1, :] = as_row(
            jnp.sum(jnp.where(picked, product, 0.0), axis=1, keepdims=True)
        )


def expert_plain(pieces, slabs, experts, count):
    gate_slab, up_slab, down_slab = slabs
    features = gate_slab.shape[0]
    rows = jnp.concatenate(pieces, axis=0).reshape(-1, 2, count, features + PAD)
    rows_x = rows[:, 0].reshape(-1, features + PAD)
    rows_dy = rows[:, 1, :, :features].reshape(-1, features)
    is_own = jnp.arange(PAD, dtype=jnp.int32)[None, :] == lax.axis_index("expert")
    weight = jnp.sum(
        jnp.where(is_own, rows_x[:, features:].astype(F32), 0.0), axis=1, keepdims=True
    )
    rows_x = rows_x[:, :features]
    pre_gate = jnp.dot(rows_x, gate_slab, preferred_element_type=F32)
    pre_up = jnp.dot(rows_x, up_slab, preferred_element_type=F32)
    back = contract_last(rows_dy, down_slab)
    sig = jax.nn.sigmoid(pre_gate)
    active = pre_gate * sig
    hidden = (active * pre_up).astype(BF)
    d_hidden = weight * back
    d_gate = (d_hidden * pre_up * (sig * (1.0 + pre_gate * (1.0 - sig)))).astype(BF)
    d_up = (d_hidden * active).astype(BF)
    scaled = (weight * rows_dy.astype(F32)).astype(BF)
    product = jnp.sum(hidden.astype(F32) * back, axis=1, keepdims=True)
    half = product.shape[0] // 2
    part = contract_last(d_gate, gate_slab) + contract_last(d_up, up_slab)
    wide = jnp.concatenate([part, jnp.where(is_own, product, 0.0)], axis=1)
    send = to_wire(wide[half:], experts)
    return rows_x, scaled, hidden, d_gate, d_up, send, wide[:half]


def to_wire(total, experts):
    pad = total[:, -PAD:]
    rest = jnp.roll(pad - lax.reduce_precision(pad, 8, 7), experts, 1)
    lane = jnp.arange(PAD)[None, :]
    pad = jnp.where((lane >= experts) & (lane < 2 * experts), pad + rest, pad)
    return jnp.concatenate([total[:, :-PAD], pad], axis=1).astype(BF)


def sum_plain(keep, parts, pieces, stays, experts):
    for part in parts:
        keep = keep + part.astype(F32)
    split = jnp.split(keep, pieces, axis=0)
    return [
        piece if stays and i == 0 else to_wire(piece, experts) for i, piece in enumerate(split)
    ]


def expert_step(pieces, weights, experts, count, limit, load):
    w_gate, w_up, w_down = weights
    rows = sum(piece.shape[0] for piece in pieces) // 2
    features, hidden_units = w_gate.shape[1:]
    width = features + PAD
    if rows > limit:
        return *expert_plain(pieces, (w_gate[0], w_up[0], w_down[0]), experts, count), *weights
    outs = [
        shape((rows, features), BF),
        shape((rows, features), BF),
        shape((rows, hidden_units), BF),
        shape((rows, hidden_units), BF),
        shape((rows, hidden_units), BF),
        shape((rows // 2, width), BF),
        shape((rows // 2, width), F32),
    ]
    scratch = [pltpu.VMEM((rows, features), BF), pltpu.VMEM((rows, PAD), F32)]
    weight_space = pltpu.VMEM
    if load:
        outs += [shape(w.shape, BF) for w in weights]
        scratch.append(pltpu.SemaphoreType.DMA((3,)))
        weight_space = pltpu.HBM
    specs = [pl.BlockSpec(memory_space=pltpu.VMEM)] * len(pieces)
    result = pl.pallas_call(
        functools.partial(expert_body, experts, count, load, len(pieces)),
        out_shape=outs,
        in_specs=specs + [pl.BlockSpec(memory_space=weight_space)] * 3,
        scratch_shapes=scratch,
        name="expert",
        compiler_params=pltpu.CompilerParams(vmem_limit_bytes=(44 if load else 24) * MIB),
        cost_estimate=pl.CostEstimate(
            flops=0,
            bytes_accessed=1024,
            transcendentals=0,
        ),
    )(*pieces, *weights)
    return result if load else [*result, *weights]


def local(tokens, upstream, route_ids, route_gates, w_gate, w_up, w_down):
    experts = lax.axis_size("expert")
    groups = lax.axis_size("section") // 2
    count, features = tokens.shape
    width = features + PAD
    fits = 2 * experts * groups * count <= LARGEST
    ids, gates = route_ids.T, route_gates.T

    block = pl.pallas_call(
        pack_body,
        out_shape=shape((2 * count, width), BF),
        in_specs=[pl.BlockSpec(memory_space=pltpu.HBM)] * 4,
        scratch_shapes=[
            pltpu.VMEM(tokens.shape, BF),
            pltpu.VMEM(tokens.shape, BF),
            pltpu.VMEM(ids.shape, jnp.int32),
            pltpu.VMEM(ids.shape, BF),
            pltpu.SemaphoreType.DMA((4,)),
        ],
        name="pack",
        compiler_params=pltpu.CompilerParams(vmem_limit_bytes=32 * MIB),
    )(*[pltpu.with_memory_space_constraint(v, pltpu.HBM) for v in (tokens, upstream, ids, gates)])

    def to_others(value):
        return [value] + [swap(value, "expert", d) for d in range(1, experts)]

    def added(total, parts, pieces, stays, name):
        if fits:
            return sum_parts(total, parts, pieces, stays, experts, name)
        return sum_plain(total, parts, pieces, stays, experts)

    others = sorted(range(1, experts), key=lambda d: -d.bit_count())
    along = [swap(block, "section", 2 * k) for k in range(groups - 1, 1, -1)][::-1]
    near = [swap(block, "expert", d) for d in others]
    far_block = jnp.concatenate(along, axis=0)
    near_block = jnp.concatenate([block] + near, axis=0)
    far_block, near_block = lax.optimization_barrier((far_block, near_block))
    far = [swap(far_block, "expert", d) for d in others[1:]]
    far += [swap(near_block, "section", 2), swap(far_block, "expert", others[0])]

    limit = LARGEST if fits else 0
    order = [(0, 0)] + [(d, 0) for d in others] + [(0, k) for k in range(2, groups)]
    mine = jnp.concatenate([near_block, far_block], axis=0)
    *first, w_gate, w_up, w_down = expert_step(
        [mine, swap(mine, "section", 1)], (w_gate, w_up, w_down), experts, count, limit, True
    )
    order += [(d, k) for d in others[1:] for k in range(2, groups)]
    order += [(0, 1)] + [(d, 1) for d in others]
    order += [(others[0], k) for k in range(2, groups)]
    mine = far
    mine, first[5] = lax.optimization_barrier((mine, first[5]))
    second = expert_step(
        mine + [swap(piece, "section", 1) for piece in mine],
        (w_gate, w_up, w_down),
        experts,
        count,
        limit,
        False,
    )[:7]
    steps = [first, second]
    sends = [swap(step[5], "section", 1) for step in steps]
    keeps = [step[6] for step in steps]
    groups_of = [
        [(d, 0) for d in range(experts)],
        [(0, k) for k in range(2, groups)],
        [(d, 1) for d in range(experts)],
    ] + [[(d, k) for k in range(2, groups)] for d in others]
    where = [[order.index(item) for item in items] for items in groups_of]
    if fits:
        split = pl.pallas_call(
            functools.partial(join_body, experts, count, where),
            out_shape=[
                shape((len(items) * count, width), F32 if i < 2 else BF)
                for i, items in enumerate(where)
            ],
            scratch_shapes=[pltpu.VMEM((experts * groups * count, width), F32)],
            name="sum_cores",
            compiler_params=pltpu.CompilerParams(vmem_limit_bytes=VMEM),
            cost_estimate=pl.CostEstimate(flops=0, bytes_accessed=1024, transcendentals=0),
        )(*keeps, *sends)
    else:
        total = jnp.concatenate(keeps, axis=0) + jnp.concatenate(sends, axis=0).astype(F32)
        blocks = total.reshape(-1, count, width)
        split = [jnp.concatenate([blocks[i] for i in places], axis=0) for places in where]
        split = split[:2] + [to_wire(part, experts) for part in split[2:]]
    crossed = [swap(part, "expert", d) for d, part in zip(others, split[3:])]
    beside = swap(split[2], "section", 2)
    own, *sideways = added(split[0], [beside], experts, True, "sum_near")
    onward = added(split[1], crossed, groups - 2, False, "sum_far")
    parts = [swap(part, "expert", d) for d, part in enumerate(sideways, 1)]
    parts += [swap(part, "section", 2 * k) for k, part in enumerate(onward, 2)]
    grad_tokens, grad_gates = call(
        functools.partial(final_body, experts, len(parts)),
        [shape((count, features), BF), shape(ids.shape, F32)],
        "final",
        0,
        4 * count * width * 2,
    )(own, *parts, ids)

    rows_x, scaled, hidden, d_gate, d_up = [
        jnp.concatenate(both, axis=0) for both in list(zip(*steps))[:5]
    ]
    grad_down = contract_first(hidden, scaled)
    grad_gate = contract_first(rows_x, d_gate)
    grad_up = contract_first(rows_x, d_up)
    return (
        grad_tokens,
        grad_gates.T,
        grad_gate.astype(BF)[None],
        grad_up.astype(BF)[None],
        grad_down.astype(BF)[None],
    )


def solution(mesh):
    placed = (
        P(("section", "expert"), None),
        P(("section", "expert"), None),
        P(("section", "expert"), None),
        P(("section", "expert"), None),
        P("expert", None, "section"),
        P("expert", None, "section"),
        P("expert", "section", None),
    )
    return jax.shard_map(
        local,
        mesh=mesh,
        in_specs=placed,
        out_specs=(
            P(("section", "expert"), None),
            P(("section", "expert"), None),
            P("expert", None, "section"),
            P("expert", None, "section"),
            P("expert", "section", None),
        ),
        check_vma=False,
    )
```

```python
import functools

import jax
import jax.numpy as jnp
from jax import lax
from jax.experimental import pallas as pl
from jax.experimental.pallas import tpu as pltpu
from jax.sharding import PartitionSpec as P

PAD = 128
MIB = 1024 * 1024
VMEM = 28 * MIB
LARGEST = 256
PARTS = 4
BF = jnp.bfloat16
F32 = jnp.float32


def contract_last(left, right):
    return lax.dot_general(
        left, right, (((1,), (1,)), ((), ())), preferred_element_type=jnp.float32
    )


def contract_first(left, right):
    return lax.dot_general(
        left, right, (((0,), (0,)), ((), ())), preferred_element_type=jnp.float32
    )


def swap(value, axis, mask):
    size = lax.axis_size(axis)
    return lax.ppermute(value, axis, [(i, i ^ mask) for i in range(size)])


def call(body, outs, name, flops=0, moved=0):
    return pl.pallas_call(
        body,
        out_shape=outs,
        name=name,
        compiler_params=pltpu.CompilerParams(vmem_limit_bytes=VMEM),
        cost_estimate=pl.CostEstimate(flops=flops, bytes_accessed=moved, transcendentals=0),
    )


def shape(dims, dtype):
    return jax.ShapeDtypeStruct(dims, dtype)


def lanes(rows):
    return lax.broadcasted_iota(jnp.int32, (rows, PAD), 1)


def wire_pad(total, experts):
    lane = lanes(total.shape[0])
    rest = total - total.astype(BF).astype(F32)
    low = (lane >= experts) & (lane < 2 * experts)
    return jnp.where(low, total + pltpu.roll(rest, experts, 1), total).astype(BF)


def column(row):
    count = row.shape[1]
    here = lax.broadcasted_iota(jnp.int32, (count, count), 0)
    there = lax.broadcasted_iota(jnp.int32, (count, count), 1)
    return jnp.sum(jnp.where(here == there, row, 0.0), axis=1, keepdims=True)


def as_row(col):
    count = col.shape[0]
    here = lax.broadcasted_iota(jnp.int32, (count, count), 0)
    there = lax.broadcasted_iota(jnp.int32, (count, count), 1)
    return jnp.sum(jnp.where(here == there, col, 0.0), axis=0, keepdims=True)


def pack_body(x_hbm, dy_hbm, ids_hbm, gates_hbm, out_ref, x_ref, dy_ref, ids_ref, gates_ref, sems):
    pairs = ((ids_hbm, ids_ref), (gates_hbm, gates_ref), (x_hbm, x_ref), (dy_hbm, dy_ref))
    copies = [pltpu.make_async_copy(src, dst, sems.at[i]) for i, (src, dst) in enumerate(pairs)]
    for copy in copies:
        copy.start()
    for copy in copies:
        copy.wait()
    count, features = x_ref.shape
    lane = lanes(count).astype(F32)
    gates = gates_ref[...].astype(F32)
    ids = ids_ref[...].astype(F32)
    dense = jnp.zeros((count, PAD), F32)
    for k in range(ids.shape[0]):
        dense = jnp.where(lane == column(ids[k : k + 1]), column(gates[k : k + 1]), dense)
    out_ref[:, :features] = jnp.concatenate(
        [x_ref[...].astype(F32), dy_ref[...].astype(F32)], axis=0
    ).astype(BF)
    out_ref[:, features:] = jnp.concatenate([dense, dense], axis=0).astype(BF)


def weights_body(gate_hbm, up_hbm, down_hbm, out_ref, stage_ref, sems):
    units = stage_ref.shape[0]
    places = (stage_ref, out_ref.at[:, :units], out_ref.at[:, units : 2 * units])
    copies = []
    for i, (src, dst) in enumerate(zip((down_hbm, gate_hbm, up_hbm), places)):
        copies.append(pltpu.make_async_copy(src.at[0], dst, sems.at[i]))
        copies[i].start()
    for copy in copies:
        copy.wait()
    out_ref[:, 2 * units :] = stage_ref[...].T


def back_body(own_ref, other_ref, out_ref):
    both = own_ref.shape[1] // 3 * 2
    out_ref[:both, :] = own_ref[:, :both].T
    out_ref[both:, :] = other_ref[:, :both].T


def expert_body(experts, count, pieces_count, *refs):
    pieces, (own_ref, other_ref, back_ref) = refs[:pieces_count], refs[pieces_count : pieces_count + 3]
    *sums, pass_ref, acts_ref, x_ref, dy_ref, weight_ref = refs[pieces_count + 3 :]
    features = x_ref.shape[1]
    units = own_ref.shape[1] // 3
    own = lax.axis_index("expert")

    blocks = [(piece, at) for piece in pieces for at in range(0, piece.shape[0], 2 * count)]
    lane = lanes(2 * count)
    for i in range(0, len(blocks), 2):
        halves = [ref[at : at + 2 * count, :].astype(F32) for ref, at in blocks[i : i + 2]]
        rows = pl.ds(i * count, 2 * count)
        x = jnp.concatenate([h[:count, :features] for h in halves], axis=0).astype(BF)
        dy = jnp.concatenate([h[count:, :features] for h in halves], axis=0)
        dense = jnp.concatenate([h[:count, features:] for h in halves], axis=0)
        weight = jnp.sum(jnp.where(lane == own, dense, 0.0), axis=1, keepdims=True)
        weight_ref[rows, :] = jnp.broadcast_to(weight, (2 * count, PAD))
        x_ref[rows, :] = x
        dy_ref[rows, :] = dy.astype(BF)
        pass_ref[rows, :features] = x
        pass_ref[rows, features : 2 * features] = (weight * dy).astype(BF)

    grads = []
    product = 0.0
    for ref in (own_ref, other_ref):
        both = jnp.dot(x_ref[...], ref[:, : 2 * units], preferred_element_type=F32)
        pre_gate, pre_up = both[:, :units], both[:, units:]
        back = jnp.dot(dy_ref[...], ref[:, 2 * units :], preferred_element_type=F32)
        sig = jax.nn.sigmoid(pre_gate)
        active = pre_gate * sig
        hidden = (active * pre_up).astype(BF)
        d_hidden = weight_ref[:, :1] * back
        d_gate = (d_hidden * pre_up * (sig * (1.0 + pre_gate * (1.0 - sig)))).astype(BF)
        d_up = (d_hidden * active).astype(BF)
        product = product + jnp.sum(hidden.astype(F32) * back, axis=1, keepdims=True)
        grads += [d_gate, d_up]
        if ref is own_ref:
            acts_ref[...] = jnp.concatenate([hidden, d_gate, d_up], axis=1)
        else:
            pass_ref[:, 2 * features :] = jnp.concatenate([hidden, d_gate, d_up], axis=1)
    part = jnp.dot(jnp.concatenate(grads, axis=1), back_ref[...], preferred_element_type=F32)
    spread = jnp.where(lanes(part.shape[0]) == own, product, 0.0)
    at = 0
    for out in sums:
        rows = slice(at, at + out.shape[0])
        at += out.shape[0]
        out[:, :features] = part[rows].astype(out.dtype)
        if out.dtype == F32:
            out[:, features:] = spread[rows]
        else:
            out[:, features:] = wire_pad(spread[rows], experts)


def grads_body(parts, pass_ref, got_ref, acts_ref, *refs):
    gate_hbm, up_hbm, down_hbm, x_ref, scaled_ref, all_ref, gate_ref, up_ref, down_ref, sems = refs
    half, features = pass_ref.shape[0], x_ref.shape[1]
    units = acts_ref.shape[1] // 3
    for i, ref in enumerate((pass_ref, got_ref)):
        rows = pl.ds(i * half, half)
        x_ref[rows, :] = ref[:, :features]
        scaled_ref[rows, :] = ref[:, features : 2 * features]
    all_ref[:half, :] = acts_ref[...]
    all_ref[half:, :] = got_ref[:, 2 * features :]
    step = features // parts
    copies = []
    for i in range(parts):
        at = pl.ds(i * step, step)
        both = contract_first(x_ref[:, at], all_ref[:, units:])
        gate_ref[at, :] = both[:, :units].astype(BF)
        up_ref[at, :] = both[:, units:].astype(BF)
        down_ref[:, at] = contract_first(all_ref[:, :units], scaled_ref[:, at]).astype(BF)
        for j, (src, dst) in enumerate(
            (
                (gate_ref.at[at, :], gate_hbm.at[0, at, :]),
                (up_ref.at[at, :], up_hbm.at[0, at, :]),
                (down_ref.at[:, at], down_hbm.at[0, :, at]),
            )
        ):
            copies.append(pltpu.make_async_copy(src, dst, sems.at[i, j]))
            copies[-1].start()
    for copy in copies:
        copy.wait()


def sum_body(experts, added, stays, *refs):
    keep_ref, parts, outs = refs[0], refs[1 : 1 + added], refs[1 + added :]
    rows, width = outs[0].shape
    for i, out in enumerate(outs):
        at = pl.ds(i * rows, rows)
        total = keep_ref[at, :]
        for part in parts:
            total = total + part[at, :].astype(F32)
        if i == 0 and stays:
            out[...] = total
        else:
            out[:, : width - PAD] = total[:, : width - PAD].astype(BF)
            out[:, width - PAD :] = wire_pad(total[:, width - PAD :], experts)


def sum_parts(keep, parts, pieces, stays, experts, name):
    rows = keep.shape[0] // pieces
    dims = (rows, keep.shape[1])
    outs = [shape(dims, F32 if stays and i == 0 else BF) for i in range(pieces)]
    moved = 2 * keep.size * (2 + len(parts))
    return call(
        functools.partial(sum_body, experts, len(parts), stays),
        outs,
        name,
        keep.size * len(parts),
        moved,
    )(keep, *parts)


def final_body(experts, added, *refs):
    keep_ref, parts, (ids_ref, tokens_ref, gates_ref) = refs[0], refs[1 : 1 + added], refs[1 + added :]
    count, features = tokens_ref.shape
    total = keep_ref[...]
    for part in parts:
        total = total + part[...].astype(F32)
    tokens_ref[...] = total[:, :features].astype(BF)
    product = total[:, features:]
    lane = lanes(count).astype(F32)
    ids = ids_ref[...].astype(F32)
    for k in range(ids.shape[0]):
        id_k = column(ids[k : k + 1])
        picked = (lane == id_k) | (lane == id_k + experts)
        gates_ref[k : k + 1, :] = as_row(
            jnp.sum(jnp.where(picked, product, 0.0), axis=1, keepdims=True)
        )


def to_wire(total, experts):
    pad = total[:, -PAD:]
    rest = jnp.roll(pad - lax.reduce_precision(pad, 8, 7), experts, 1)
    lane = jnp.arange(PAD)[None, :]
    pad = jnp.where((lane >= experts) & (lane < 2 * experts), pad + rest, pad)
    return jnp.concatenate([total[:, :-PAD], pad], axis=1).astype(BF)


def sum_plain(keep, parts, pieces, stays, experts):
    for part in parts:
        keep = keep + part.astype(F32)
    split = jnp.split(keep, pieces, axis=0)
    return [
        piece if stays and i == 0 else to_wire(piece, experts) for i, piece in enumerate(split)
    ]


def expert_plain(pieces, own_slabs, other_slabs, experts, count, sizes):
    features = own_slabs.shape[0]
    units = own_slabs.shape[1] // 3
    rows = jnp.concatenate(pieces, axis=0).reshape(-1, 2, count, features + PAD)
    rows_x = rows[:, 0].reshape(-1, features + PAD)
    rows_dy = rows[:, 1, :, :features].reshape(-1, features)
    is_own = jnp.arange(PAD, dtype=jnp.int32)[None, :] == lax.axis_index("expert")
    weight = jnp.sum(
        jnp.where(is_own, rows_x[:, features:].astype(F32), 0.0), axis=1, keepdims=True
    )
    rows_x = rows_x[:, :features]
    scaled = (weight * rows_dy.astype(F32)).astype(BF)
    part = product = 0.0
    acts = []
    for slabs in (own_slabs, other_slabs):
        both = jnp.dot(rows_x, slabs[:, : 2 * units], preferred_element_type=F32)
        pre_gate, pre_up = both[:, :units], both[:, units:]
        back = jnp.dot(rows_dy, slabs[:, 2 * units :], preferred_element_type=F32)
        sig = jax.nn.sigmoid(pre_gate)
        active = pre_gate * sig
        hidden = (active * pre_up).astype(BF)
        d_hidden = weight * back
        d_gate = (d_hidden * pre_up * (sig * (1.0 + pre_gate * (1.0 - sig)))).astype(BF)
        d_up = (d_hidden * active).astype(BF)
        product = product + jnp.sum(hidden.astype(F32) * back, axis=1, keepdims=True)
        part = part + contract_last(jnp.concatenate([d_gate, d_up], axis=1), slabs[:, : 2 * units])
        acts.append(jnp.concatenate([hidden, d_gate, d_up], axis=1))
    wide = jnp.concatenate([part, jnp.where(is_own, product, 0.0)], axis=1)
    sums = []
    at = 0
    for rows, dtype in sizes:
        piece = wide[at : at + rows]
        at += rows
        sums.append(piece if dtype == F32 else to_wire(piece, experts))
    return *sums, jnp.concatenate([rows_x, scaled, acts[1]], axis=1), acts[0]


def local(tokens, upstream, route_ids, route_gates, w_gate, w_up, w_down):
    experts = lax.axis_size("expert")
    groups = lax.axis_size("section") // 2
    count, features = tokens.shape
    units = w_gate.shape[2]
    width = features + PAD
    rows = experts * groups * count
    fits = 2 * rows <= LARGEST
    ids, gates = route_ids.T, route_gates.T

    def in_hbm(*values):
        return [pltpu.with_memory_space_constraint(v, pltpu.HBM) for v in values]

    block = pl.pallas_call(
        pack_body,
        out_shape=shape((2 * count, width), BF),
        in_specs=[pl.BlockSpec(memory_space=pltpu.HBM)] * 4,
        scratch_shapes=[
            pltpu.VMEM(tokens.shape, BF),
            pltpu.VMEM(tokens.shape, BF),
            pltpu.VMEM(ids.shape, jnp.int32),
            pltpu.VMEM(ids.shape, BF),
            pltpu.SemaphoreType.DMA((4,)),
        ],
        name="pack",
        compiler_params=pltpu.CompilerParams(vmem_limit_bytes=VMEM),
    )(*in_hbm(tokens, upstream, ids, gates))

    def added(total, parts, pieces, stays, name):
        if fits:
            return sum_parts(total, parts, pieces, stays, experts, name)
        return sum_plain(total, parts, pieces, stays, experts)

    others = sorted(range(1, experts), key=lambda d: -d.bit_count())
    along = [swap(block, "section", 2 * k) for k in range(groups - 1, 1, -1)][::-1]
    near = [swap(block, "expert", d) for d in others]
    far_block = jnp.concatenate(along, axis=0)
    near_block = jnp.concatenate([block] + near, axis=0)

    if fits:
        slabs = pl.pallas_call(
            weights_body,
            out_shape=shape((features, 3 * units), BF),
            in_specs=[pl.BlockSpec(memory_space=pltpu.HBM)] * 3,
            scratch_shapes=[pltpu.VMEM((units, features), BF), pltpu.SemaphoreType.DMA((3,))],
            name="weights",
            compiler_params=pltpu.CompilerParams(vmem_limit_bytes=VMEM),
            cost_estimate=pl.CostEstimate(flops=0, bytes_accessed=1024, transcendentals=0),
        )(*in_hbm(w_gate, w_up, w_down))
    else:
        slabs = jnp.concatenate([w_gate[0], w_up[0], w_down[0].T], axis=1)
    far_block, near_block, slabs = lax.optimization_barrier((far_block, near_block, slabs))
    other_slabs = swap(slabs, "section", 1)

    far = [swap(far_block, "expert", d) for d in others[1:]]
    far += [swap(near_block, "section", 2), swap(far_block, "expert", others[0])]
    *direct, beside, diagonal = far
    pieces = [near_block, far_block, beside, diagonal, *direct]
    sizes = [(experts * count, F32), ((groups - 2) * count, F32), (experts * count, BF)]
    sizes += [((groups - 2) * count, BF)] * len(others)
    if fits:
        back_slabs = call(back_body, shape((4 * units, features), BF), "back")(slabs, other_slabs)
        *split, passed, acts = pl.pallas_call(
            functools.partial(expert_body, experts, count, len(pieces)),
            out_shape=[shape((size, width), dtype) for size, dtype in sizes]
            + [shape((rows, 2 * features + 3 * units), BF), shape((rows, 3 * units), BF)],
            scratch_shapes=[
                pltpu.VMEM((rows, features), BF),
                pltpu.VMEM((rows, features), BF),
                pltpu.VMEM((rows, PAD), F32),
            ],
            name="expert",
            compiler_params=pltpu.CompilerParams(vmem_limit_bytes=VMEM),
            cost_estimate=pl.CostEstimate(flops=0, bytes_accessed=1024, transcendentals=0),
        )(*pieces, slabs, other_slabs, back_slabs)
    else:
        *split, passed, acts = expert_plain(pieces, slabs, other_slabs, experts, count, sizes)

    got = swap(passed, "section", 1)
    if fits:
        grad_gate, grad_up, grad_down = pl.pallas_call(
            functools.partial(grads_body, PARTS),
            out_shape=[shape(w.shape, BF) for w in (w_gate, w_up, w_down)],
            out_specs=[pl.BlockSpec(memory_space=pltpu.HBM)] * 3,
            scratch_shapes=[
                pltpu.VMEM((2 * rows, features), BF),
                pltpu.VMEM((2 * rows, features), BF),
                pltpu.VMEM((2 * rows, 3 * units), BF),
                pltpu.VMEM((features, units), BF),
                pltpu.VMEM((features, units), BF),
                pltpu.VMEM((units, features), BF),
                pltpu.SemaphoreType.DMA((PARTS, 3)),
            ],
            name="grads",
            compiler_params=pltpu.CompilerParams(vmem_limit_bytes=VMEM),
            cost_estimate=pl.CostEstimate(flops=0, bytes_accessed=1024, transcendentals=0),
        )(passed, got, acts)
    else:
        every = jnp.concatenate([passed, got], axis=0)
        acts = jnp.concatenate([acts, got[:, 2 * features :]], axis=0)
        hidden, d_gate, d_up = jnp.split(acts, 3, axis=1)
        rows_x, scaled = every[:, :features], every[:, features : 2 * features]
        grad_gate = contract_first(rows_x, d_gate).astype(BF)[None]
        grad_up = contract_first(rows_x, d_up).astype(BF)[None]
        grad_down = contract_first(hidden, scaled).astype(BF)[None]

    crossed = [swap(part, "expert", d) for d, part in zip(others, split[3:])]
    beside = swap(split[2], "section", 2)
    crossed, beside, grad_gate = lax.optimization_barrier((crossed, beside, grad_gate))
    own, *sideways = added(split[0], [beside], experts, True, "sum_near")
    onward = added(split[1], crossed, groups - 2, False, "sum_far")
    parts = [swap(part, "expert", d) for d, part in zip(others, sideways)]
    parts += [swap(part, "section", 2 * k) for k, part in enumerate(onward, 2)]
    grad_tokens, grad_gates = call(
        functools.partial(final_body, experts, len(parts)),
        [shape((count, features), BF), shape(ids.shape, F32)],
        "final",
        0,
        4 * count * width * 2,
    )(own, *parts, ids)

    return (
        grad_tokens,
        grad_gates.T,
        grad_gate,
        grad_up,
        grad_down,
    )


def solution(mesh):
    placed = (
        P(("section", "expert"), None),
        P(("section", "expert"), None),
        P(("section", "expert"), None),
        P(("section", "expert"), None),
        P("expert", None, "section"),
        P("expert", None, "section"),
        P("expert", "section", None),
    )
    return jax.shard_map(
        local,
        mesh=mesh,
        in_specs=placed,
        out_specs=(
            P(("section", "expert"), None),
            P(("section", "expert"), None),
            P("expert", None, "section"),
            P("expert", None, "section"),
            P("expert", "section", None),
        ),
        check_vma=False,
    )
```

```python
import functools

import jax
import jax.numpy as jnp
from jax import lax
from jax.experimental import pallas as pl
from jax.experimental.pallas import tpu as pltpu
from jax.sharding import PartitionSpec as P

PAD = 128
MIB = 1024 * 1024
VMEM = 28 * MIB
LARGEST = 256
PARTS = 4
BF = jnp.bfloat16
F32 = jnp.float32


def contract_last(left, right):
    return lax.dot_general(
        left, right, (((1,), (1,)), ((), ())), preferred_element_type=jnp.float32
    )


def contract_first(left, right):
    return lax.dot_general(
        left, right, (((0,), (0,)), ((), ())), preferred_element_type=jnp.float32
    )


def swap(value, axis, mask):
    size = lax.axis_size(axis)
    return lax.ppermute(value, axis, [(i, i ^ mask) for i in range(size)])


def call(body, outs, name, flops=0, moved=0):
    return pl.pallas_call(
        body,
        out_shape=outs,
        name=name,
        compiler_params=pltpu.CompilerParams(vmem_limit_bytes=VMEM),
        cost_estimate=pl.CostEstimate(flops=flops, bytes_accessed=moved, transcendentals=0),
    )


def shape(dims, dtype):
    return jax.ShapeDtypeStruct(dims, dtype)


def lanes(rows):
    return lax.broadcasted_iota(jnp.int32, (rows, PAD), 1)


def wire_pad(total, experts):
    lane = lanes(total.shape[0])
    rest = total - total.astype(BF).astype(F32)
    low = (lane >= experts) & (lane < 2 * experts)
    return jnp.where(low, total + pltpu.roll(rest, experts, 1), total).astype(BF)


def column(row):
    count = row.shape[1]
    here = lax.broadcasted_iota(jnp.int32, (count, count), 0)
    there = lax.broadcasted_iota(jnp.int32, (count, count), 1)
    return jnp.sum(jnp.where(here == there, row, 0.0), axis=1, keepdims=True)


def as_row(col):
    count = col.shape[0]
    here = lax.broadcasted_iota(jnp.int32, (count, count), 0)
    there = lax.broadcasted_iota(jnp.int32, (count, count), 1)
    return jnp.sum(jnp.where(here == there, col, 0.0), axis=0, keepdims=True)


def pack_body(x_hbm, dy_hbm, ids_hbm, gates_hbm, out_ref, ids_ref, gates_ref, sems):
    count, features = x_hbm.shape
    places = (ids_ref, gates_ref, out_ref.at[:, :features], out_ref.at[:, features : 2 * features])
    copies = []
    for i, (src, dst) in enumerate(zip((ids_hbm, gates_hbm, x_hbm, dy_hbm), places)):
        copies.append(pltpu.make_async_copy(src, dst, sems.at[i]))
        copies[i].start()
    copies[0].wait()
    copies[1].wait()
    lane = lanes(count).astype(F32)
    gates = gates_ref[...].astype(F32)
    ids = ids_ref[...].astype(F32)
    dense = jnp.zeros((count, PAD), F32)
    for k in range(ids.shape[0]):
        dense = jnp.where(lane == column(ids[k : k + 1]), column(gates[k : k + 1]), dense)
    out_ref[:, 2 * features :] = dense.astype(BF)
    copies[2].wait()
    copies[3].wait()


def weights_body(gate_hbm, up_hbm, down_hbm, out_ref, stage_ref, sems):
    units = stage_ref.shape[0]
    places = (stage_ref, out_ref.at[:, :units], out_ref.at[:, units : 2 * units])
    copies = []
    for i, (src, dst) in enumerate(zip((down_hbm, gate_hbm, up_hbm), places)):
        copies.append(pltpu.make_async_copy(src.at[0], dst, sems.at[i]))
        copies[i].start()
    for copy in copies:
        copy.wait()
    out_ref[:, 2 * units :] = stage_ref[...].T


def back_body(own_ref, other_ref, out_ref):
    both = own_ref.shape[1] // 3 * 2
    out_ref[:both, :] = own_ref[:, :both].T
    out_ref[both:, :] = other_ref[:, :both].T


def expert_body(experts, pieces_count, *refs):
    pieces, (own_ref, other_ref, back_ref) = refs[:pieces_count], refs[pieces_count : pieces_count + 3]
    *sums, pass_ref, acts_ref, dy_ref, weight_ref = refs[pieces_count + 3 :]
    features = dy_ref.shape[1]
    units = own_ref.shape[1] // 3
    own = lax.axis_index("expert")

    at = 0
    for piece in pieces:
        rows = pl.ds(at, piece.shape[0])
        at += piece.shape[0]
        dense = piece[:, 2 * features :].astype(F32)
        weight = jnp.sum(jnp.where(lanes(piece.shape[0]) == own, dense, 0.0), axis=1, keepdims=True)
        weight_ref[rows, :] = jnp.broadcast_to(weight, dense.shape)
        dy = piece[:, features : 2 * features]
        dy_ref[rows, :] = dy
        pass_ref[rows, :features] = piece[:, :features]
        pass_ref[rows, features : 2 * features] = (weight * dy.astype(F32)).astype(BF)

    grads = []
    product = 0.0
    for ref in (own_ref, other_ref):
        both = jnp.dot(
            pass_ref[:, :features], ref[:, : 2 * units], preferred_element_type=F32
        )
        pre_gate, pre_up = both[:, :units], both[:, units:]
        back = jnp.dot(dy_ref[...], ref[:, 2 * units :], preferred_element_type=F32)
        sig = jax.nn.sigmoid(pre_gate)
        active = pre_gate * sig
        hidden = (active * pre_up).astype(BF)
        d_hidden = weight_ref[:, :1] * back
        d_gate = (d_hidden * pre_up * (sig * (1.0 + pre_gate * (1.0 - sig)))).astype(BF)
        d_up = (d_hidden * active).astype(BF)
        product = product + jnp.sum(hidden.astype(F32) * back, axis=1, keepdims=True)
        grads += [d_gate, d_up]
        if ref is own_ref:
            acts_ref[...] = jnp.concatenate([hidden, d_gate, d_up], axis=1)
        else:
            pass_ref[:, 2 * features :] = jnp.concatenate([hidden, d_gate, d_up], axis=1)
    part = jnp.dot(jnp.concatenate(grads, axis=1), back_ref[...], preferred_element_type=F32)
    spread = jnp.where(lanes(part.shape[0]) == own, product, 0.0)
    at = 0
    for out in sums:
        rows = slice(at, at + out.shape[0])
        at += out.shape[0]
        out[:, :features] = part[rows].astype(out.dtype)
        if out.dtype == F32:
            out[:, features:] = spread[rows]
        else:
            out[:, features:] = wire_pad(spread[rows], experts)


def grads_body(parts, pass_ref, got_ref, acts_ref, *refs):
    gate_hbm, up_hbm, down_hbm, x_ref, scaled_ref, all_ref, gate_ref, up_ref, down_ref, sems = refs
    half, features = pass_ref.shape[0], x_ref.shape[1]
    units = acts_ref.shape[1] // 3
    for i, ref in enumerate((pass_ref, got_ref)):
        rows = pl.ds(i * half, half)
        x_ref[rows, :] = ref[:, :features]
        scaled_ref[rows, :] = ref[:, features : 2 * features]
    all_ref[:half, :] = acts_ref[...]
    all_ref[half:, :] = got_ref[:, 2 * features :]
    step = features // parts
    copies = []
    for i in range(parts):
        at = pl.ds(i * step, step)
        both = contract_first(x_ref[:, at], all_ref[:, units:])
        gate_ref[at, :] = both[:, :units].astype(BF)
        up_ref[at, :] = both[:, units:].astype(BF)
        down_ref[:, at] = contract_first(all_ref[:, :units], scaled_ref[:, at]).astype(BF)
        for j, (src, dst) in enumerate(
            (
                (gate_ref.at[at, :], gate_hbm.at[0, at, :]),
                (up_ref.at[at, :], up_hbm.at[0, at, :]),
                (down_ref.at[:, at], down_hbm.at[0, :, at]),
            )
        ):
            copies.append(pltpu.make_async_copy(src, dst, sems.at[i, j]))
            copies[-1].start()
    for copy in copies:
        copy.wait()


def sum_body(experts, added, stays, *refs):
    keep_ref, parts, outs = refs[0], refs[1 : 1 + added], refs[1 + added :]
    rows, width = outs[0].shape
    for i, out in enumerate(outs):
        at = pl.ds(i * rows, rows)
        total = keep_ref[at, :]
        for part in parts:
            total = total + part[at, :].astype(F32)
        if i == 0 and stays:
            out[...] = total
        else:
            out[:, : width - PAD] = total[:, : width - PAD].astype(BF)
            out[:, width - PAD :] = wire_pad(total[:, width - PAD :], experts)


def sum_parts(keep, parts, pieces, stays, experts, name):
    rows = keep.shape[0] // pieces
    dims = (rows, keep.shape[1])
    outs = [shape(dims, F32 if stays and i == 0 else BF) for i in range(pieces)]
    moved = 2 * keep.size * (2 + len(parts))
    return call(
        functools.partial(sum_body, experts, len(parts), stays),
        outs,
        name,
        keep.size * len(parts),
        moved,
    )(keep, *parts)


def final_body(experts, added, *refs):
    keep_ref, parts, (ids_ref, tokens_ref, gates_ref) = refs[0], refs[1 : 1 + added], refs[1 + added :]
    count, features = tokens_ref.shape
    total = keep_ref[...]
    for part in parts:
        total = total + part[...].astype(F32)
    tokens_ref[...] = total[:, :features].astype(BF)
    product = total[:, features:]
    lane = lanes(count).astype(F32)
    ids = ids_ref[...].astype(F32)
    for k in range(ids.shape[0]):
        id_k = column(ids[k : k + 1])
        picked = (lane == id_k) | (lane == id_k + experts)
        gates_ref[k : k + 1, :] = as_row(
            jnp.sum(jnp.where(picked, product, 0.0), axis=1, keepdims=True)
        )


def to_wire(total, experts):
    pad = total[:, -PAD:]
    rest = jnp.roll(pad - lax.reduce_precision(pad, 8, 7), experts, 1)
    lane = jnp.arange(PAD)[None, :]
    pad = jnp.where((lane >= experts) & (lane < 2 * experts), pad + rest, pad)
    return jnp.concatenate([total[:, :-PAD], pad], axis=1).astype(BF)


def sum_plain(keep, parts, pieces, stays, experts):
    for part in parts:
        keep = keep + part.astype(F32)
    split = jnp.split(keep, pieces, axis=0)
    return [
        piece if stays and i == 0 else to_wire(piece, experts) for i, piece in enumerate(split)
    ]


def expert_plain(pieces, own_slabs, other_slabs, experts, sizes):
    features = own_slabs.shape[0]
    units = own_slabs.shape[1] // 3
    rows = jnp.concatenate(pieces, axis=0)
    rows_x, rows_dy = rows[:, :features], rows[:, features : 2 * features]
    is_own = jnp.arange(PAD, dtype=jnp.int32)[None, :] == lax.axis_index("expert")
    weight = jnp.sum(
        jnp.where(is_own, rows[:, 2 * features :].astype(F32), 0.0), axis=1, keepdims=True
    )
    scaled = (weight * rows_dy.astype(F32)).astype(BF)
    part = product = 0.0
    acts = []
    for slabs in (own_slabs, other_slabs):
        both = jnp.dot(rows_x, slabs[:, : 2 * units], preferred_element_type=F32)
        pre_gate, pre_up = both[:, :units], both[:, units:]
        back = jnp.dot(rows_dy, slabs[:, 2 * units :], preferred_element_type=F32)
        sig = jax.nn.sigmoid(pre_gate)
        active = pre_gate * sig
        hidden = (active * pre_up).astype(BF)
        d_hidden = weight * back
        d_gate = (d_hidden * pre_up * (sig * (1.0 + pre_gate * (1.0 - sig)))).astype(BF)
        d_up = (d_hidden * active).astype(BF)
        product = product + jnp.sum(hidden.astype(F32) * back, axis=1, keepdims=True)
        part = part + contract_last(jnp.concatenate([d_gate, d_up], axis=1), slabs[:, : 2 * units])
        acts.append(jnp.concatenate([hidden, d_gate, d_up], axis=1))
    wide = jnp.concatenate([part, jnp.where(is_own, product, 0.0)], axis=1)
    sums = []
    at = 0
    for rows, dtype in sizes:
        piece = wide[at : at + rows]
        at += rows
        sums.append(piece if dtype == F32 else to_wire(piece, experts))
    return *sums, jnp.concatenate([rows_x, scaled, acts[1]], axis=1), acts[0]


def local(tokens, upstream, route_ids, route_gates, w_gate, w_up, w_down):
    experts = lax.axis_size("expert")
    groups = lax.axis_size("section") // 2
    count, features = tokens.shape
    units = w_gate.shape[2]
    width = features + PAD
    rows = experts * groups * count
    fits = 2 * rows <= LARGEST
    ids, gates = route_ids.T, route_gates.T

    def in_hbm(*values):
        return [pltpu.with_memory_space_constraint(v, pltpu.HBM) for v in values]

    block = pl.pallas_call(
        pack_body,
        out_shape=shape((count, 2 * features + PAD), BF),
        in_specs=[pl.BlockSpec(memory_space=pltpu.HBM)] * 4,
        scratch_shapes=[
            pltpu.VMEM(ids.shape, jnp.int32),
            pltpu.VMEM(ids.shape, BF),
            pltpu.SemaphoreType.DMA((4,)),
        ],
        name="pack",
        compiler_params=pltpu.CompilerParams(vmem_limit_bytes=VMEM),
    )(*in_hbm(tokens, upstream, ids, gates))

    def added(total, parts, pieces, stays, name):
        if fits:
            return sum_parts(total, parts, pieces, stays, experts, name)
        return sum_plain(total, parts, pieces, stays, experts)

    others = sorted(range(1, experts), key=lambda d: -d.bit_count())
    along = [swap(block, "section", 2 * k) for k in range(groups - 1, 1, -1)][::-1]
    near = [swap(block, "expert", d) for d in others]
    far_block = jnp.concatenate(along, axis=0)
    near_block = jnp.concatenate([block] + near, axis=0)

    if fits:
        slabs = pl.pallas_call(
            weights_body,
            out_shape=shape((features, 3 * units), BF),
            in_specs=[pl.BlockSpec(memory_space=pltpu.HBM)] * 3,
            scratch_shapes=[pltpu.VMEM((units, features), BF), pltpu.SemaphoreType.DMA((3,))],
            name="weights",
            compiler_params=pltpu.CompilerParams(vmem_limit_bytes=VMEM),
            cost_estimate=pl.CostEstimate(flops=0, bytes_accessed=1024, transcendentals=0),
        )(*in_hbm(w_gate, w_up, w_down))
    else:
        slabs = jnp.concatenate([w_gate[0], w_up[0], w_down[0].T], axis=1)
    far_block, near_block, slabs = lax.optimization_barrier((far_block, near_block, slabs))
    other_slabs = swap(slabs, "section", 1)

    far = [swap(far_block, "expert", d) for d in others[1:]]
    far += [swap(near_block, "section", 2), swap(far_block, "expert", others[0])]
    *direct, beside, diagonal = far
    pieces = [near_block, far_block, beside, *direct, diagonal]
    sizes = [(experts * count, F32), ((groups - 2) * count, F32), (experts * count, BF)]
    sizes += [((groups - 2) * count, BF)] * len(others)
    if fits:
        back_slabs = call(back_body, shape((4 * units, features), BF), "back")(slabs, other_slabs)
        *split, passed, acts = pl.pallas_call(
            functools.partial(expert_body, experts, len(pieces)),
            out_shape=[shape((size, width), dtype) for size, dtype in sizes]
            + [shape((rows, 2 * features + 3 * units), BF), shape((rows, 3 * units), BF)],
            scratch_shapes=[
                pltpu.VMEM((rows, features), BF),
                pltpu.VMEM((rows, PAD), F32),
            ],
            name="expert",
            compiler_params=pltpu.CompilerParams(vmem_limit_bytes=VMEM),
            cost_estimate=pl.CostEstimate(flops=0, bytes_accessed=1024, transcendentals=0),
        )(*pieces, slabs, other_slabs, back_slabs)
    else:
        *split, passed, acts = expert_plain(pieces, slabs, other_slabs, experts, sizes)

    got = swap(passed, "section", 1)
    if fits:
        grad_gate, grad_up, grad_down = pl.pallas_call(
            functools.partial(grads_body, PARTS),
            out_shape=[shape(w.shape, BF) for w in (w_gate, w_up, w_down)],
            out_specs=[pl.BlockSpec(memory_space=pltpu.HBM)] * 3,
            scratch_shapes=[
                pltpu.VMEM((2 * rows, features), BF),
                pltpu.VMEM((2 * rows, features), BF),
                pltpu.VMEM((2 * rows, 3 * units), BF),
                pltpu.VMEM((features, units), BF),
                pltpu.VMEM((features, units), BF),
                pltpu.VMEM((units, features), BF),
                pltpu.SemaphoreType.DMA((PARTS, 3)),
            ],
            name="grads",
            compiler_params=pltpu.CompilerParams(vmem_limit_bytes=VMEM),
            cost_estimate=pl.CostEstimate(flops=0, bytes_accessed=1024, transcendentals=0),
        )(passed, got, acts)
    else:
        every = jnp.concatenate([passed, got], axis=0)
        acts = jnp.concatenate([acts, got[:, 2 * features :]], axis=0)
        hidden, d_gate, d_up = jnp.split(acts, 3, axis=1)
        rows_x, scaled = every[:, :features], every[:, features : 2 * features]
        grad_gate = contract_first(rows_x, d_gate).astype(BF)[None]
        grad_up = contract_first(rows_x, d_up).astype(BF)[None]
        grad_down = contract_first(hidden, scaled).astype(BF)[None]

    crossed = [
        swap(part, "expert", d) for d, part in zip(others, [split[-1], *split[3:-1]])
    ]
    beside = swap(split[2], "section", 2)
    crossed, beside, grad_gate = lax.optimization_barrier((crossed, beside, grad_gate))
    own, *sideways = added(split[0], [beside], experts, True, "sum_near")
    onward = added(split[1], crossed, groups - 2, False, "sum_far")
    parts = [swap(part, "expert", d) for d, part in zip(others, sideways)]
    parts += [swap(part, "section", 2 * k) for k, part in enumerate(onward, 2)]
    grad_tokens, grad_gates = call(
        functools.partial(final_body, experts, len(parts)),
        [shape((count, features), BF), shape(ids.shape, F32)],
        "final",
        0,
        4 * count * width * 2,
    )(own, *parts, ids)

    return (
        grad_tokens,
        grad_gates.T,
        grad_gate,
        grad_up,
        grad_down,
    )


def solution(mesh):
    placed = (
        P(("section", "expert"), None),
        P(("section", "expert"), None),
        P(("section", "expert"), None),
        P(("section", "expert"), None),
        P("expert", None, "section"),
        P("expert", None, "section"),
        P("expert", "section", None),
    )
    return jax.shard_map(
        local,
        mesh=mesh,
        in_specs=placed,
        out_specs=(
            P(("section", "expert"), None),
            P(("section", "expert"), None),
            P("expert", None, "section"),
            P("expert", None, "section"),
            P("expert", "section", None),
        ),
        check_vma=False,
    )
```

```python
import functools

import jax
import jax.numpy as jnp
from jax import lax
from jax.experimental import pallas as pl
from jax.experimental.pallas import tpu as pltpu
from jax.sharding import PartitionSpec as P

PAD = 128
MIB = 1024 * 1024
VMEM = 28 * MIB
LARGEST = 256
COST = 4 * 10**9
LONG = ("sum_far", "sum_along")
PARTS = 4
BF = jnp.bfloat16
F32 = jnp.float32


def contract_last(left, right):
    return lax.dot_general(
        left, right, (((1,), (1,)), ((), ())), preferred_element_type=jnp.float32
    )


def contract_first(left, right):
    return lax.dot_general(
        left, right, (((0,), (0,)), ((), ())), preferred_element_type=jnp.float32
    )


def swap(value, axis, mask):
    size = lax.axis_size(axis)
    return lax.ppermute(value, axis, [(i, i ^ mask) for i in range(size)])


def call(body, outs, name, flops=0, moved=0):
    return pl.pallas_call(
        body,
        out_shape=outs,
        name=name,
        compiler_params=pltpu.CompilerParams(vmem_limit_bytes=VMEM),
        cost_estimate=pl.CostEstimate(flops=flops, bytes_accessed=moved, transcendentals=0),
    )


def shape(dims, dtype):
    return jax.ShapeDtypeStruct(dims, dtype)


def lanes(rows):
    return lax.broadcasted_iota(jnp.int32, (rows, PAD), 1)


def wire_pad(total, experts):
    lane = lanes(total.shape[0])
    rest = total - total.astype(BF).astype(F32)
    low = (lane >= experts) & (lane < 2 * experts)
    return jnp.where(low, total + pltpu.roll(rest, experts, 1), total).astype(BF)


def column(row):
    count = row.shape[1]
    here = lax.broadcasted_iota(jnp.int32, (count, count), 0)
    there = lax.broadcasted_iota(jnp.int32, (count, count), 1)
    return jnp.sum(jnp.where(here == there, row, 0.0), axis=1, keepdims=True)


def as_row(col):
    count = col.shape[0]
    here = lax.broadcasted_iota(jnp.int32, (count, count), 0)
    there = lax.broadcasted_iota(jnp.int32, (count, count), 1)
    return jnp.sum(jnp.where(here == there, col, 0.0), axis=0, keepdims=True)


def pack_body(x_hbm, dy_hbm, ids_hbm, gates_hbm, out_ref, ids_ref, gates_ref, sems):
    count, features = x_hbm.shape
    places = (ids_ref, gates_ref, out_ref.at[:, :features], out_ref.at[:, features : 2 * features])
    copies = []
    for i, (src, dst) in enumerate(zip((ids_hbm, gates_hbm, x_hbm, dy_hbm), places)):
        copies.append(pltpu.make_async_copy(src, dst, sems.at[i]))
        copies[i].start()
    copies[0].wait()
    copies[1].wait()
    lane = lanes(count).astype(F32)
    gates = gates_ref[...].astype(F32)
    ids = ids_ref[...].astype(F32)
    dense = jnp.zeros((count, PAD), F32)
    for k in range(ids.shape[0]):
        dense = jnp.where(lane == column(ids[k : k + 1]), column(gates[k : k + 1]), dense)
    out_ref[:, 2 * features :] = dense.astype(BF)
    copies[2].wait()
    copies[3].wait()


def weights_body(gate_hbm, up_hbm, down_hbm, out_ref, stage_ref, sems):
    units = stage_ref.shape[0]
    places = (stage_ref, out_ref.at[:, :units], out_ref.at[:, units : 2 * units])
    copies = []
    for i, (src, dst) in enumerate(zip((down_hbm, gate_hbm, up_hbm), places)):
        copies.append(pltpu.make_async_copy(src.at[0], dst, sems.at[i]))
        copies[i].start()
    for copy in copies:
        copy.wait()
    out_ref[:, 2 * units :] = stage_ref[...].T


def back_body(own_ref, other_ref, out_ref):
    both = own_ref.shape[1] // 3 * 2
    out_ref[:both, :] = own_ref[:, :both].T
    out_ref[both:, :] = other_ref[:, :both].T


def expert_body(experts, pieces_count, *refs):
    pieces, (own_ref, other_ref, back_ref) = refs[:pieces_count], refs[pieces_count : pieces_count + 3]
    *sums, pass_ref, acts_ref, dy_ref, weight_ref = refs[pieces_count + 3 :]
    features = dy_ref.shape[1]
    units = own_ref.shape[1] // 3
    own = lax.axis_index("expert")

    at = 0
    for piece in pieces:
        rows = pl.ds(at, piece.shape[0])
        at += piece.shape[0]
        dense = piece[:, 2 * features :].astype(F32)
        weight = jnp.sum(jnp.where(lanes(piece.shape[0]) == own, dense, 0.0), axis=1, keepdims=True)
        weight_ref[rows, :] = jnp.broadcast_to(weight, dense.shape)
        dy = piece[:, features : 2 * features]
        dy_ref[rows, :] = dy
        pass_ref[rows, :features] = piece[:, :features]
        pass_ref[rows, features : 2 * features] = (weight * dy.astype(F32)).astype(BF)

    grads = []
    product = 0.0
    for ref in (own_ref, other_ref):
        both = jnp.dot(
            pass_ref[:, :features], ref[:, : 2 * units], preferred_element_type=F32
        )
        pre_gate, pre_up = both[:, :units], both[:, units:]
        back = jnp.dot(dy_ref[...], ref[:, 2 * units :], preferred_element_type=F32)
        sig = jax.nn.sigmoid(pre_gate)
        active = pre_gate * sig
        hidden = (active * pre_up).astype(BF)
        d_hidden = weight_ref[:, :1] * back
        d_gate = (d_hidden * pre_up * (sig * (1.0 + pre_gate * (1.0 - sig)))).astype(BF)
        d_up = (d_hidden * active).astype(BF)
        product = product + jnp.sum(hidden.astype(F32) * back, axis=1, keepdims=True)
        grads += [d_gate, d_up]
        if ref is own_ref:
            acts_ref[...] = jnp.concatenate([hidden, d_gate, d_up], axis=1)
        else:
            pass_ref[:, 2 * features :] = jnp.concatenate([hidden, d_gate, d_up], axis=1)
    part = jnp.dot(jnp.concatenate(grads, axis=1), back_ref[...], preferred_element_type=F32)
    spread = jnp.where(lanes(part.shape[0]) == own, product, 0.0)
    at = 0
    for out in sums:
        rows = slice(at, at + out.shape[0])
        at += out.shape[0]
        out[:, :features] = part[rows].astype(out.dtype)
        if out.dtype == F32:
            out[:, features:] = spread[rows]
        else:
            out[:, features:] = wire_pad(spread[rows], experts)


def grads_body(parts, pass_ref, got_ref, acts_ref, *refs):
    gate_hbm, up_hbm, down_hbm, x_ref, scaled_ref, all_ref, gate_ref, up_ref, down_ref, sems = refs
    half, features = pass_ref.shape[0], x_ref.shape[1]
    units = acts_ref.shape[1] // 3
    for i, ref in enumerate((pass_ref, got_ref)):
        rows = pl.ds(i * half, half)
        x_ref[rows, :] = ref[:, :features]
        scaled_ref[rows, :] = ref[:, features : 2 * features]
    all_ref[:half, :] = acts_ref[...]
    all_ref[half:, :] = got_ref[:, 2 * features :]
    step = features // parts
    copies = []
    for i in range(parts):
        at = pl.ds(i * step, step)
        both = contract_first(x_ref[:, at], all_ref[:, units:])
        gate_ref[at, :] = both[:, :units].astype(BF)
        up_ref[at, :] = both[:, units:].astype(BF)
        down_ref[:, at] = contract_first(all_ref[:, :units], scaled_ref[:, at]).astype(BF)
        for j, (src, dst) in enumerate(
            (
                (gate_ref.at[at, :], gate_hbm.at[0, at, :]),
                (up_ref.at[at, :], up_hbm.at[0, at, :]),
                (down_ref.at[:, at], down_hbm.at[0, :, at]),
            )
        ):
            copies.append(pltpu.make_async_copy(src, dst, sems.at[i, j]))
            copies[-1].start()
    for copy in copies:
        copy.wait()


def sum_body(experts, added, stays, *refs):
    keep_ref, parts, outs = refs[0], refs[1 : 1 + added], refs[1 + added :]
    rows, width = outs[0].shape
    for i, out in enumerate(outs):
        at = pl.ds(i * rows, rows)
        total = keep_ref[at, :]
        for part in parts:
            total = total + part[at, :].astype(F32)
        if i == 0 and stays:
            out[...] = total
        else:
            out[:, : width - PAD] = total[:, : width - PAD].astype(BF)
            out[:, width - PAD :] = wire_pad(total[:, width - PAD :], experts)


def sum_parts(keep, parts, pieces, stays, experts, name):
    rows = keep.shape[0] // pieces
    dims = (rows, keep.shape[1])
    outs = [shape(dims, F32 if stays and i == 0 else BF) for i in range(pieces)]
    return call(
        functools.partial(sum_body, experts, len(parts), stays),
        outs,
        name,
        COST if name in LONG else 0,
        1024,
    )(keep, *parts)


def final_body(experts, added, *refs):
    keep_ref, parts, (ids_ref, tokens_ref, gates_ref) = refs[0], refs[1 : 1 + added], refs[1 + added :]
    count, features = tokens_ref.shape
    total = keep_ref[...]
    for part in parts:
        total = total + part[...].astype(F32)
    tokens_ref[...] = total[:, :features].astype(BF)
    product = total[:, features:]
    lane = lanes(count).astype(F32)
    ids = ids_ref[...].astype(F32)
    for k in range(ids.shape[0]):
        id_k = column(ids[k : k + 1])
        picked = (lane == id_k) | (lane == id_k + experts)
        gates_ref[k : k + 1, :] = as_row(
            jnp.sum(jnp.where(picked, product, 0.0), axis=1, keepdims=True)
        )


def to_wire(total, experts):
    pad = total[:, -PAD:]
    rest = jnp.roll(pad - lax.reduce_precision(pad, 8, 7), experts, 1)
    lane = jnp.arange(PAD)[None, :]
    pad = jnp.where((lane >= experts) & (lane < 2 * experts), pad + rest, pad)
    return jnp.concatenate([total[:, :-PAD], pad], axis=1).astype(BF)


def sum_plain(keep, parts, pieces, stays, experts):
    for part in parts:
        keep = keep + part.astype(F32)
    split = jnp.split(keep, pieces, axis=0)
    return [
        piece if stays and i == 0 else to_wire(piece, experts) for i, piece in enumerate(split)
    ]


def expert_plain(pieces, own_slabs, other_slabs, experts, sizes):
    features = own_slabs.shape[0]
    units = own_slabs.shape[1] // 3
    rows = jnp.concatenate(pieces, axis=0)
    rows_x, rows_dy = rows[:, :features], rows[:, features : 2 * features]
    is_own = jnp.arange(PAD, dtype=jnp.int32)[None, :] == lax.axis_index("expert")
    weight = jnp.sum(
        jnp.where(is_own, rows[:, 2 * features :].astype(F32), 0.0), axis=1, keepdims=True
    )
    scaled = (weight * rows_dy.astype(F32)).astype(BF)
    part = product = 0.0
    acts = []
    for slabs in (own_slabs, other_slabs):
        both = jnp.dot(rows_x, slabs[:, : 2 * units], preferred_element_type=F32)
        pre_gate, pre_up = both[:, :units], both[:, units:]
        back = jnp.dot(rows_dy, slabs[:, 2 * units :], preferred_element_type=F32)
        sig = jax.nn.sigmoid(pre_gate)
        active = pre_gate * sig
        hidden = (active * pre_up).astype(BF)
        d_hidden = weight * back
        d_gate = (d_hidden * pre_up * (sig * (1.0 + pre_gate * (1.0 - sig)))).astype(BF)
        d_up = (d_hidden * active).astype(BF)
        product = product + jnp.sum(hidden.astype(F32) * back, axis=1, keepdims=True)
        part = part + contract_last(jnp.concatenate([d_gate, d_up], axis=1), slabs[:, : 2 * units])
        acts.append(jnp.concatenate([hidden, d_gate, d_up], axis=1))
    wide = jnp.concatenate([part, jnp.where(is_own, product, 0.0)], axis=1)
    sums = []
    at = 0
    for rows, dtype in sizes:
        piece = wide[at : at + rows]
        at += rows
        sums.append(piece if dtype == F32 else to_wire(piece, experts))
    return *sums, jnp.concatenate([rows_x, scaled, acts[1]], axis=1), acts[0]


def local(tokens, upstream, route_ids, route_gates, w_gate, w_up, w_down):
    experts = lax.axis_size("expert")
    groups = lax.axis_size("section") // 2
    count, features = tokens.shape
    units = w_gate.shape[2]
    width = features + PAD
    rows = experts * groups * count
    fits = 2 * rows <= LARGEST
    ids, gates = route_ids.T, route_gates.T

    def in_hbm(*values):
        return [pltpu.with_memory_space_constraint(v, pltpu.HBM) for v in values]

    block = pl.pallas_call(
        pack_body,
        out_shape=shape((count, 2 * features + PAD), BF),
        in_specs=[pl.BlockSpec(memory_space=pltpu.HBM)] * 4,
        scratch_shapes=[
            pltpu.VMEM(ids.shape, jnp.int32),
            pltpu.VMEM(ids.shape, BF),
            pltpu.SemaphoreType.DMA((4,)),
        ],
        name="pack",
        compiler_params=pltpu.CompilerParams(vmem_limit_bytes=VMEM),
    )(*in_hbm(tokens, upstream, ids, gates))

    def added(total, parts, pieces, stays, name):
        if fits:
            return sum_parts(total, parts, pieces, stays, experts, name)
        return sum_plain(total, parts, pieces, stays, experts)

    others = sorted(range(1, experts), key=lambda d: -d.bit_count())
    along = [swap(block, "section", 2 * k) for k in range(groups - 1, 1, -1)]
    close = others[::-1]
    near = [swap(block, "expert", d) for d in close]
    far_block = jnp.concatenate(along, axis=0)
    near_block = jnp.concatenate([block] + near, axis=0)

    if fits:
        slabs = pl.pallas_call(
            weights_body,
            out_shape=shape((features, 3 * units), BF),
            in_specs=[pl.BlockSpec(memory_space=pltpu.HBM)] * 3,
            scratch_shapes=[pltpu.VMEM((units, features), BF), pltpu.SemaphoreType.DMA((3,))],
            name="weights",
            compiler_params=pltpu.CompilerParams(vmem_limit_bytes=VMEM),
            cost_estimate=pl.CostEstimate(flops=0, bytes_accessed=1024, transcendentals=0),
        )(*in_hbm(w_gate, w_up, w_down))
    else:
        slabs = jnp.concatenate([w_gate[0], w_up[0], w_down[0].T], axis=1)
    far_block, near_block, slabs = lax.optimization_barrier((far_block, near_block, slabs))
    other_slabs = swap(slabs, "section", 1)

    far = [swap(far_block, "expert", d) for d in others[1:]]
    far += [swap(near_block, "section", 2), swap(far_block, "expert", others[0])]
    *direct, beside, diagonal = far
    pieces = [near_block, far_block, beside, *direct, diagonal]
    sizes = [(experts * count, F32), ((groups - 2) * count, F32), (experts * count, BF)]
    sizes += [((groups - 2) * count, BF)] * len(others)
    if fits:
        back_slabs = call(back_body, shape((4 * units, features), BF), "back")(slabs, other_slabs)
        *split, passed, acts = pl.pallas_call(
            functools.partial(expert_body, experts, len(pieces)),
            out_shape=[shape((size, width), dtype) for size, dtype in sizes]
            + [shape((rows, 2 * features + 3 * units), BF), shape((rows, 3 * units), BF)],
            scratch_shapes=[
                pltpu.VMEM((rows, features), BF),
                pltpu.VMEM((rows, PAD), F32),
            ],
            name="expert",
            compiler_params=pltpu.CompilerParams(vmem_limit_bytes=VMEM),
            cost_estimate=pl.CostEstimate(flops=0, bytes_accessed=1024, transcendentals=0),
        )(*pieces, slabs, other_slabs, back_slabs)
    else:
        *split, passed, acts = expert_plain(pieces, slabs, other_slabs, experts, sizes)

    got = swap(passed, "section", 1)
    if fits:
        grad_gate, grad_up, grad_down = pl.pallas_call(
            functools.partial(grads_body, PARTS),
            out_shape=[shape(w.shape, BF) for w in (w_gate, w_up, w_down)],
            out_specs=[pl.BlockSpec(memory_space=pltpu.HBM)] * 3,
            scratch_shapes=[
                pltpu.VMEM((2 * rows, features), BF),
                pltpu.VMEM((2 * rows, features), BF),
                pltpu.VMEM((2 * rows, 3 * units), BF),
                pltpu.VMEM((features, units), BF),
                pltpu.VMEM((features, units), BF),
                pltpu.VMEM((units, features), BF),
                pltpu.SemaphoreType.DMA((PARTS, 3)),
            ],
            name="grads",
            compiler_params=pltpu.CompilerParams(vmem_limit_bytes=VMEM),
            cost_estimate=pl.CostEstimate(flops=0, bytes_accessed=1024, transcendentals=0),
        )(passed, got, acts)
    else:
        every = jnp.concatenate([passed, got], axis=0)
        acts = jnp.concatenate([acts, got[:, 2 * features :]], axis=0)
        hidden, d_gate, d_up = jnp.split(acts, 3, axis=1)
        rows_x, scaled = every[:, :features], every[:, features : 2 * features]
        grad_gate = contract_first(rows_x, d_gate).astype(BF)[None]
        grad_up = contract_first(rows_x, d_up).astype(BF)[None]
        grad_down = contract_first(hidden, scaled).astype(BF)[None]

    crossed = [
        swap(part, "expert", d) for d, part in zip(others, [split[-1], *split[3:-1]])
    ]
    beside = swap(split[2], "section", 2)
    crossed, grad_gate = lax.optimization_barrier((crossed, grad_gate))
    onward = added(split[1], crossed, groups - 2, False, "sum_far")
    own, *sideways = added(split[0], [beside], experts, True, "sum_near")
    ahead = dict(zip(range(groups - 1, 1, -1), onward))
    along = [swap(ahead[k], "section", 2 * k) for k in range(2, groups)]
    (own,) = added(own, along, 1, True, "sum_along")
    around = dict(zip(close, sideways))
    parts = [swap(around[d], "expert", d) for d in others]
    grad_tokens, grad_gates = call(
        functools.partial(final_body, experts, len(parts)),
        [shape((count, features), BF), shape(ids.shape, F32)],
        "final",
        0,
        4 * count * width * 2,
    )(own, *parts, ids)

    return (
        grad_tokens,
        grad_gates.T,
        grad_gate,
        grad_up,
        grad_down,
    )


def solution(mesh):
    placed = (
        P(("section", "expert"), None),
        P(("section", "expert"), None),
        P(("section", "expert"), None),
        P(("section", "expert"), None),
        P("expert", None, "section"),
        P("expert", None, "section"),
        P("expert", "section", None),
    )
    return jax.shard_map(
        local,
        mesh=mesh,
        in_specs=placed,
        out_specs=(
            P(("section", "expert"), None),
            P(("section", "expert"), None),
            P("expert", None, "section"),
            P("expert", None, "section"),
            P("expert", "section", None),
        ),
        check_vma=False,
    )
```

```python
import functools

import jax
import jax.numpy as jnp
from jax import lax
from jax.experimental import pallas as pl
from jax.experimental.pallas import tpu as pltpu
from jax.sharding import PartitionSpec as P

PAD = 128
MIB = 1024 * 1024
VMEM = 28 * MIB
LARGEST = 256
COST = 4 * 10**9
LONG = ("sum_far", "sum_along")
PARTS = 4
BF = jnp.bfloat16
F32 = jnp.float32


def contract_last(left, right):
    return lax.dot_general(
        left, right, (((1,), (1,)), ((), ())), preferred_element_type=jnp.float32
    )


def contract_first(left, right):
    return lax.dot_general(
        left, right, (((0,), (0,)), ((), ())), preferred_element_type=jnp.float32
    )


def swap(value, axis, mask):
    size = lax.axis_size(axis)
    return lax.ppermute(value, axis, [(i, i ^ mask) for i in range(size)])


def call(body, outs, name, flops=0, moved=0):
    return pl.pallas_call(
        body,
        out_shape=outs,
        name=name,
        compiler_params=pltpu.CompilerParams(vmem_limit_bytes=VMEM),
        cost_estimate=pl.CostEstimate(flops=flops, bytes_accessed=moved, transcendentals=0),
    )


def shape(dims, dtype):
    return jax.ShapeDtypeStruct(dims, dtype)


def lanes(rows):
    return lax.broadcasted_iota(jnp.int32, (rows, PAD), 1)


def wire_pad(total, experts):
    lane = lanes(total.shape[0])
    rest = total - total.astype(BF).astype(F32)
    low = (lane >= experts) & (lane < 2 * experts)
    return jnp.where(low, total + pltpu.roll(rest, experts, 1), total).astype(BF)


def column(row):
    count = row.shape[1]
    here = lax.broadcasted_iota(jnp.int32, (count, count), 0)
    there = lax.broadcasted_iota(jnp.int32, (count, count), 1)
    return jnp.sum(jnp.where(here == there, row, 0.0), axis=1, keepdims=True)


def as_row(col):
    count = col.shape[0]
    here = lax.broadcasted_iota(jnp.int32, (count, count), 0)
    there = lax.broadcasted_iota(jnp.int32, (count, count), 1)
    return jnp.sum(jnp.where(here == there, col, 0.0), axis=0, keepdims=True)


def pack_body(x_hbm, dy_hbm, ids_hbm, gates_hbm, out_ref, ids_ref, gates_ref, sems):
    count, features = x_hbm.shape
    places = (ids_ref, gates_ref, out_ref.at[:, :features], out_ref.at[:, features : 2 * features])
    copies = []
    for i, (src, dst) in enumerate(zip((ids_hbm, gates_hbm, x_hbm, dy_hbm), places)):
        copies.append(pltpu.make_async_copy(src, dst, sems.at[i]))
        copies[i].start()
    copies[0].wait()
    copies[1].wait()
    lane = lanes(count).astype(F32)
    gates = gates_ref[...].astype(F32)
    ids = ids_ref[...].astype(F32)
    dense = jnp.zeros((count, PAD), F32)
    for k in range(ids.shape[0]):
        dense = jnp.where(lane == column(ids[k : k + 1]), column(gates[k : k + 1]), dense)
    out_ref[:, 2 * features :] = dense.astype(BF)
    copies[2].wait()
    copies[3].wait()


def weights_body(gate_hbm, up_hbm, down_hbm, out_ref, stage_ref, sems):
    units = stage_ref.shape[0]
    places = (stage_ref, out_ref.at[:, :units], out_ref.at[:, units : 2 * units])
    copies = []
    for i, (src, dst) in enumerate(zip((down_hbm, gate_hbm, up_hbm), places)):
        copies.append(pltpu.make_async_copy(src.at[0], dst, sems.at[i]))
        copies[i].start()
    for copy in copies:
        copy.wait()
    out_ref[:, 2 * units :] = stage_ref[...].T


def back_body(own_ref, other_ref, out_ref):
    both = own_ref.shape[1] // 3 * 2
    out_ref[:both, :] = own_ref[:, :both].T
    out_ref[both:, :] = other_ref[:, :both].T


def expert_body(experts, pieces_count, *refs):
    pieces, (own_ref, other_ref, back_ref) = refs[:pieces_count], refs[pieces_count : pieces_count + 3]
    *sums, pass_ref, acts_ref, weight_ref = refs[pieces_count + 3 :]
    features = own_ref.shape[0]
    width = 2 * features + PAD
    units = own_ref.shape[1] // 3
    own = lax.axis_index("expert")

    at = 0
    for piece in pieces:
        rows = pl.ds(at, piece.shape[0])
        at += piece.shape[0]
        dense = piece[:, 2 * features :].astype(F32)
        weight = jnp.sum(jnp.where(lanes(piece.shape[0]) == own, dense, 0.0), axis=1, keepdims=True)
        weight_ref[rows, :] = jnp.broadcast_to(weight, dense.shape)
        pass_ref[rows, :width] = piece[...]

    grads = []
    product = 0.0
    for ref in (own_ref, other_ref):
        both = jnp.dot(
            pass_ref[:, :features], ref[:, : 2 * units], preferred_element_type=F32
        )
        pre_gate, pre_up = both[:, :units], both[:, units:]
        back = jnp.dot(
            pass_ref[:, features : 2 * features], ref[:, 2 * units :], preferred_element_type=F32
        )
        sig = jax.nn.sigmoid(pre_gate)
        active = pre_gate * sig
        hidden = (active * pre_up).astype(BF)
        d_hidden = weight_ref[:, :1] * back
        d_gate = (d_hidden * pre_up * (sig * (1.0 + pre_gate * (1.0 - sig)))).astype(BF)
        d_up = (d_hidden * active).astype(BF)
        product = product + jnp.sum(hidden.astype(F32) * back, axis=1, keepdims=True)
        grads += [d_gate, d_up]
        if ref is own_ref:
            acts_ref[...] = jnp.concatenate([hidden, d_gate, d_up], axis=1)
        else:
            pass_ref[:, width:] = jnp.concatenate([hidden, d_gate, d_up], axis=1)
    part = jnp.dot(jnp.concatenate(grads, axis=1), back_ref[...], preferred_element_type=F32)
    spread = jnp.where(lanes(part.shape[0]) == own, product, 0.0)
    at = 0
    for out in sums:
        rows = slice(at, at + out.shape[0])
        at += out.shape[0]
        out[:, :features] = part[rows].astype(out.dtype)
        if out.dtype == F32:
            out[:, features:] = spread[rows]
        else:
            out[:, features:] = wire_pad(spread[rows], experts)


def grads_body(parts, pass_ref, got_ref, acts_ref, *refs):
    gate_hbm, up_hbm, down_hbm, x_ref, scaled_ref, all_ref, gate_ref, up_ref, down_ref, sems = refs
    half, features = pass_ref.shape[0], x_ref.shape[1]
    units = acts_ref.shape[1] // 3
    own = lax.axis_index("expert")
    for i, ref in enumerate((pass_ref, got_ref)):
        rows = pl.ds(i * half, half)
        x_ref[rows, :] = ref[:, :features]
        dense = ref[:, 2 * features : 2 * features + PAD].astype(F32)
        weight = jnp.sum(jnp.where(lanes(half) == own, dense, 0.0), axis=1, keepdims=True)
        scaled_ref[rows, :] = (weight * ref[:, features : 2 * features].astype(F32)).astype(BF)
    all_ref[:half, :] = acts_ref[...]
    all_ref[half:, :] = got_ref[:, 2 * features + PAD :]
    step = features // parts
    copies = []
    for i in range(parts):
        at = pl.ds(i * step, step)
        both = contract_first(x_ref[:, at], all_ref[:, units:])
        gate_ref[at, :] = both[:, :units].astype(BF)
        up_ref[at, :] = both[:, units:].astype(BF)
        down_ref[:, at] = contract_first(all_ref[:, :units], scaled_ref[:, at]).astype(BF)
        for j, (src, dst) in enumerate(
            (
                (gate_ref.at[at, :], gate_hbm.at[0, at, :]),
                (up_ref.at[at, :], up_hbm.at[0, at, :]),
                (down_ref.at[:, at], down_hbm.at[0, :, at]),
            )
        ):
            copies.append(pltpu.make_async_copy(src, dst, sems.at[i, j]))
            copies[-1].start()
    for copy in copies:
        copy.wait()


def sum_body(experts, added, stays, *refs):
    keep_ref, parts, outs = refs[0], refs[1 : 1 + added], refs[1 + added :]
    rows, width = outs[0].shape
    for i, out in enumerate(outs):
        at = pl.ds(i * rows, rows)
        total = keep_ref[at, :]
        for part in parts:
            total = total + part[at, :].astype(F32)
        if i == 0 and stays:
            out[...] = total
        else:
            out[:, : width - PAD] = total[:, : width - PAD].astype(BF)
            out[:, width - PAD :] = wire_pad(total[:, width - PAD :], experts)


def sum_parts(keep, parts, pieces, stays, experts, name):
    rows = keep.shape[0] // pieces
    dims = (rows, keep.shape[1])
    outs = [shape(dims, F32 if stays and i == 0 else BF) for i in range(pieces)]
    return call(
        functools.partial(sum_body, experts, len(parts), stays),
        outs,
        name,
        COST if name in LONG else 0,
        1024,
    )(keep, *parts)


def final_body(experts, added, *refs):
    keep_ref, parts, (ids_ref, tokens_ref, gates_ref) = refs[0], refs[1 : 1 + added], refs[1 + added :]
    count, features = tokens_ref.shape
    total = keep_ref[...]
    for part in parts:
        total = total + part[...].astype(F32)
    tokens_ref[...] = total[:, :features].astype(BF)
    product = total[:, features:]
    lane = lanes(count).astype(F32)
    ids = ids_ref[...].astype(F32)
    for k in range(ids.shape[0]):
        id_k = column(ids[k : k + 1])
        picked = (lane == id_k) | (lane == id_k + experts)
        gates_ref[k : k + 1, :] = as_row(
            jnp.sum(jnp.where(picked, product, 0.0), axis=1, keepdims=True)
        )


def to_wire(total, experts):
    pad = total[:, -PAD:]
    rest = jnp.roll(pad - lax.reduce_precision(pad, 8, 7), experts, 1)
    lane = jnp.arange(PAD)[None, :]
    pad = jnp.where((lane >= experts) & (lane < 2 * experts), pad + rest, pad)
    return jnp.concatenate([total[:, :-PAD], pad], axis=1).astype(BF)


def sum_plain(keep, parts, pieces, stays, experts):
    for part in parts:
        keep = keep + part.astype(F32)
    split = jnp.split(keep, pieces, axis=0)
    return [
        piece if stays and i == 0 else to_wire(piece, experts) for i, piece in enumerate(split)
    ]


def expert_plain(pieces, own_slabs, other_slabs, experts, sizes):
    features = own_slabs.shape[0]
    units = own_slabs.shape[1] // 3
    all_rows = rows = jnp.concatenate(pieces, axis=0)
    rows_x, rows_dy = rows[:, :features], rows[:, features : 2 * features]
    is_own = jnp.arange(PAD, dtype=jnp.int32)[None, :] == lax.axis_index("expert")
    weight = jnp.sum(
        jnp.where(is_own, rows[:, 2 * features :].astype(F32), 0.0), axis=1, keepdims=True
    )
    part = product = 0.0
    acts = []
    for slabs in (own_slabs, other_slabs):
        both = jnp.dot(rows_x, slabs[:, : 2 * units], preferred_element_type=F32)
        pre_gate, pre_up = both[:, :units], both[:, units:]
        back = jnp.dot(rows_dy, slabs[:, 2 * units :], preferred_element_type=F32)
        sig = jax.nn.sigmoid(pre_gate)
        active = pre_gate * sig
        hidden = (active * pre_up).astype(BF)
        d_hidden = weight * back
        d_gate = (d_hidden * pre_up * (sig * (1.0 + pre_gate * (1.0 - sig)))).astype(BF)
        d_up = (d_hidden * active).astype(BF)
        product = product + jnp.sum(hidden.astype(F32) * back, axis=1, keepdims=True)
        part = part + contract_last(jnp.concatenate([d_gate, d_up], axis=1), slabs[:, : 2 * units])
        acts.append(jnp.concatenate([hidden, d_gate, d_up], axis=1))
    wide = jnp.concatenate([part, jnp.where(is_own, product, 0.0)], axis=1)
    sums = []
    at = 0
    for rows, dtype in sizes:
        piece = wide[at : at + rows]
        at += rows
        sums.append(piece if dtype == F32 else to_wire(piece, experts))
    return *sums, jnp.concatenate([all_rows, acts[1]], axis=1), acts[0]


def local(tokens, upstream, route_ids, route_gates, w_gate, w_up, w_down):
    experts = lax.axis_size("expert")
    groups = lax.axis_size("section") // 2
    count, features = tokens.shape
    units = w_gate.shape[2]
    width = features + PAD
    rows = experts * groups * count
    fits = 2 * rows <= LARGEST
    ids, gates = route_ids.T, route_gates.T

    def in_hbm(*values):
        return [pltpu.with_memory_space_constraint(v, pltpu.HBM) for v in values]

    block = pl.pallas_call(
        pack_body,
        out_shape=shape((count, 2 * features + PAD), BF),
        in_specs=[pl.BlockSpec(memory_space=pltpu.HBM)] * 4,
        scratch_shapes=[
            pltpu.VMEM(ids.shape, jnp.int32),
            pltpu.VMEM(ids.shape, BF),
            pltpu.SemaphoreType.DMA((4,)),
        ],
        name="pack",
        compiler_params=pltpu.CompilerParams(vmem_limit_bytes=VMEM),
    )(*in_hbm(tokens, upstream, ids, gates))

    def added(total, parts, pieces, stays, name):
        if fits:
            return sum_parts(total, parts, pieces, stays, experts, name)
        return sum_plain(total, parts, pieces, stays, experts)

    others = sorted(range(1, experts), key=lambda d: -d.bit_count())
    along = [swap(block, "section", 2 * k) for k in range(groups - 1, 1, -1)]
    close = others[::-1]
    near = [swap(block, "expert", d) for d in close]
    far_block = jnp.concatenate(along, axis=0)
    near_block = jnp.concatenate([block] + near, axis=0)

    if fits:
        slabs = pl.pallas_call(
            weights_body,
            out_shape=shape((features, 3 * units), BF),
            in_specs=[pl.BlockSpec(memory_space=pltpu.HBM)] * 3,
            scratch_shapes=[pltpu.VMEM((units, features), BF), pltpu.SemaphoreType.DMA((3,))],
            name="weights",
            compiler_params=pltpu.CompilerParams(vmem_limit_bytes=VMEM),
            cost_estimate=pl.CostEstimate(flops=0, bytes_accessed=1024, transcendentals=0),
        )(*in_hbm(w_gate, w_up, w_down))
    else:
        slabs = jnp.concatenate([w_gate[0], w_up[0], w_down[0].T], axis=1)
    far_block, near_block, slabs = lax.optimization_barrier((far_block, near_block, slabs))
    other_slabs = swap(slabs, "section", 1)

    far = [swap(far_block, "expert", d) for d in others[1:]]
    far += [swap(near_block, "section", 2), swap(far_block, "expert", others[0])]
    *direct, beside, diagonal = far
    pieces = [near_block, far_block, beside, *direct, diagonal]
    sizes = [(experts * count, F32), ((groups - 2) * count, F32), (experts * count, BF)]
    sizes += [((groups - 2) * count, BF)] * len(others)
    if fits:
        back_slabs = call(back_body, shape((4 * units, features), BF), "back")(slabs, other_slabs)
        *split, passed, acts = pl.pallas_call(
            functools.partial(expert_body, experts, len(pieces)),
            out_shape=[shape((size, width), dtype) for size, dtype in sizes]
            + [shape((rows, 2 * features + PAD + 3 * units), BF), shape((rows, 3 * units), BF)],
            scratch_shapes=[
                pltpu.VMEM((rows, PAD), F32),
            ],
            name="expert",
            compiler_params=pltpu.CompilerParams(vmem_limit_bytes=VMEM),
            cost_estimate=pl.CostEstimate(flops=0, bytes_accessed=1024, transcendentals=0),
        )(*pieces, slabs, other_slabs, back_slabs)
    else:
        *split, passed, acts = expert_plain(pieces, slabs, other_slabs, experts, sizes)

    got = swap(passed, "section", 1)
    if fits:
        grad_gate, grad_up, grad_down = pl.pallas_call(
            functools.partial(grads_body, PARTS),
            out_shape=[shape(w.shape, BF) for w in (w_gate, w_up, w_down)],
            out_specs=[pl.BlockSpec(memory_space=pltpu.HBM)] * 3,
            scratch_shapes=[
                pltpu.VMEM((2 * rows, features), BF),
                pltpu.VMEM((2 * rows, features), BF),
                pltpu.VMEM((2 * rows, 3 * units), BF),
                pltpu.VMEM((features, units), BF),
                pltpu.VMEM((features, units), BF),
                pltpu.VMEM((units, features), BF),
                pltpu.SemaphoreType.DMA((PARTS, 3)),
            ],
            name="grads",
            compiler_params=pltpu.CompilerParams(vmem_limit_bytes=VMEM),
            cost_estimate=pl.CostEstimate(flops=0, bytes_accessed=1024, transcendentals=0),
        )(passed, got, acts)
    else:
        every = jnp.concatenate([passed, got], axis=0)
        acts = jnp.concatenate([acts, got[:, 2 * features + PAD :]], axis=0)
        hidden, d_gate, d_up = jnp.split(acts, 3, axis=1)
        dense = every[:, 2 * features : 2 * features + PAD].astype(F32)
        is_own = jnp.arange(PAD, dtype=jnp.int32)[None, :] == lax.axis_index("expert")
        weight = jnp.sum(jnp.where(is_own, dense, 0.0), axis=1, keepdims=True)
        rows_x = every[:, :features]
        scaled = (weight * every[:, features : 2 * features].astype(F32)).astype(BF)
        grad_gate = contract_first(rows_x, d_gate).astype(BF)[None]
        grad_up = contract_first(rows_x, d_up).astype(BF)[None]
        grad_down = contract_first(hidden, scaled).astype(BF)[None]

    crossed = [
        swap(part, "expert", d) for d, part in zip(others, [split[-1], *split[3:-1]])
    ]
    beside = swap(split[2], "section", 2)
    crossed, grad_gate = lax.optimization_barrier((crossed, grad_gate))
    onward = added(split[1], crossed, groups - 2, False, "sum_far")
    own, *sideways = added(split[0], [beside], experts, True, "sum_near")
    ahead = dict(zip(range(groups - 1, 1, -1), onward))
    along = [swap(ahead[k], "section", 2 * k) for k in range(2, groups)]
    (own,) = added(own, along, 1, True, "sum_along")
    around = dict(zip(close, sideways))
    parts = [swap(around[d], "expert", d) for d in others]
    grad_tokens, grad_gates = call(
        functools.partial(final_body, experts, len(parts)),
        [shape((count, features), BF), shape(ids.shape, F32)],
        "final",
        0,
        4 * count * width * 2,
    )(own, *parts, ids)

    return (
        grad_tokens,
        grad_gates.T,
        grad_gate,
        grad_up,
        grad_down,
    )


def solution(mesh):
    placed = (
        P(("section", "expert"), None),
        P(("section", "expert"), None),
        P(("section", "expert"), None),
        P(("section", "expert"), None),
        P("expert", None, "section"),
        P("expert", None, "section"),
        P("expert", "section", None),
    )
    return jax.shard_map(
        local,
        mesh=mesh,
        in_specs=placed,
        out_specs=(
            P(("section", "expert"), None),
            P(("section", "expert"), None),
            P("expert", None, "section"),
            P("expert", None, "section"),
            P("expert", "section", None),
        ),
        check_vma=False,
    )
```

```python
import functools

import jax
import jax.numpy as jnp
from jax import lax
from jax.experimental import pallas as pl
from jax.experimental.pallas import tpu as pltpu
from jax.sharding import PartitionSpec as P

PAD = 128
MIB = 1024 * 1024
VMEM = 28 * MIB
LARGEST = 256
COST = 4 * 10**9
LONG = ("sum_far", "sum_along")
PARTS = 6
BF = jnp.bfloat16
F32 = jnp.float32


def contract_last(left, right):
    return lax.dot_general(
        left, right, (((1,), (1,)), ((), ())), preferred_element_type=jnp.float32
    )


def contract_first(left, right):
    return lax.dot_general(
        left, right, (((0,), (0,)), ((), ())), preferred_element_type=jnp.float32
    )


def swap(value, axis, mask):
    size = lax.axis_size(axis)
    return lax.ppermute(value, axis, [(i, i ^ mask) for i in range(size)])


def call(body, outs, name, flops=0, moved=0):
    return pl.pallas_call(
        body,
        out_shape=outs,
        name=name,
        compiler_params=pltpu.CompilerParams(vmem_limit_bytes=VMEM),
        cost_estimate=pl.CostEstimate(flops=flops, bytes_accessed=moved, transcendentals=0),
    )


def shape(dims, dtype):
    return jax.ShapeDtypeStruct(dims, dtype)


def lanes(rows):
    return lax.broadcasted_iota(jnp.int32, (rows, PAD), 1)


def wire_pad(total, experts):
    lane = lanes(total.shape[0])
    rest = total - total.astype(BF).astype(F32)
    low = (lane >= experts) & (lane < 2 * experts)
    return jnp.where(low, total + pltpu.roll(rest, experts, 1), total).astype(BF)


def column(row):
    count = row.shape[1]
    here = lax.broadcasted_iota(jnp.int32, (count, count), 0)
    there = lax.broadcasted_iota(jnp.int32, (count, count), 1)
    return jnp.sum(jnp.where(here == there, row, 0.0), axis=1, keepdims=True)


def as_row(col):
    count = col.shape[0]
    here = lax.broadcasted_iota(jnp.int32, (count, count), 0)
    there = lax.broadcasted_iota(jnp.int32, (count, count), 1)
    return jnp.sum(jnp.where(here == there, col, 0.0), axis=0, keepdims=True)


def pack_body(x_hbm, dy_hbm, ids_hbm, gates_hbm, out_ref, ids_ref, gates_ref, sems):
    count, features = x_hbm.shape
    places = (ids_ref, gates_ref, out_ref.at[:, :features], out_ref.at[:, features : 2 * features])
    copies = []
    for i, (src, dst) in enumerate(zip((ids_hbm, gates_hbm, x_hbm, dy_hbm), places)):
        copies.append(pltpu.make_async_copy(src, dst, sems.at[i]))
        copies[i].start()
    copies[0].wait()
    copies[1].wait()
    lane = lanes(count).astype(F32)
    gates = gates_ref[...].astype(F32)
    ids = ids_ref[...].astype(F32)
    dense = jnp.zeros((count, PAD), F32)
    for k in range(ids.shape[0]):
        dense = jnp.where(lane == column(ids[k : k + 1]), column(gates[k : k + 1]), dense)
    out_ref[:, 2 * features :] = dense.astype(BF)
    copies[2].wait()
    copies[3].wait()


def weights_body(gate_hbm, up_hbm, down_hbm, out_ref, stage_ref, sems):
    units = stage_ref.shape[0]
    places = (stage_ref, out_ref.at[:, :units], out_ref.at[:, units : 2 * units])
    copies = []
    for i, (src, dst) in enumerate(zip((down_hbm, gate_hbm, up_hbm), places)):
        copies.append(pltpu.make_async_copy(src.at[0], dst, sems.at[i]))
        copies[i].start()
    for copy in copies:
        copy.wait()
    out_ref[:, 2 * units :] = stage_ref[...].T


def back_body(own_ref, other_ref, out_ref):
    both = own_ref.shape[1] // 3 * 2
    out_ref[:both, :] = own_ref[:, :both].T
    out_ref[both:, :] = other_ref[:, :both].T


def expert_body(experts, pieces_count, *refs):
    pieces, (own_ref, other_ref, back_ref) = refs[:pieces_count], refs[pieces_count : pieces_count + 3]
    *sums, pass_ref, acts_ref, dy_ref, weight_ref = refs[pieces_count + 3 :]
    features = dy_ref.shape[1]
    units = own_ref.shape[1] // 3
    own = lax.axis_index("expert")

    at = 0
    for piece in pieces:
        rows = pl.ds(at, piece.shape[0])
        at += piece.shape[0]
        dense = piece[:, 2 * features :].astype(F32)
        weight = jnp.sum(jnp.where(lanes(piece.shape[0]) == own, dense, 0.0), axis=1, keepdims=True)
        weight_ref[rows, :] = jnp.broadcast_to(weight, dense.shape)
        dy = piece[:, features : 2 * features]
        dy_ref[rows, :] = dy
        pass_ref[rows, :features] = piece[:, :features]
        pass_ref[rows, features : 2 * features] = (weight * dy.astype(F32)).astype(BF)

    grads = []
    product = 0.0
    for ref in (own_ref, other_ref):
        both = jnp.dot(
            pass_ref[:, :features], ref[:, : 2 * units], preferred_element_type=F32
        )
        pre_gate, pre_up = both[:, :units], both[:, units:]
        back = jnp.dot(dy_ref[...], ref[:, 2 * units :], preferred_element_type=F32)
        sig = jax.nn.sigmoid(pre_gate)
        active = pre_gate * sig
        hidden = (active * pre_up).astype(BF)
        d_hidden = weight_ref[:, :1] * back
        d_gate = (d_hidden * pre_up * (sig * (1.0 + pre_gate * (1.0 - sig)))).astype(BF)
        d_up = (d_hidden * active).astype(BF)
        product = product + jnp.sum(hidden.astype(F32) * back, axis=1, keepdims=True)
        grads += [d_gate, d_up]
        if ref is own_ref:
            acts_ref[...] = jnp.concatenate([hidden, d_gate, d_up], axis=1)
        else:
            pass_ref[:, 2 * features :] = jnp.concatenate([hidden, d_gate, d_up], axis=1)
    part = jnp.dot(jnp.concatenate(grads, axis=1), back_ref[...], preferred_element_type=F32)
    spread = jnp.where(lanes(part.shape[0]) == own, product, 0.0)
    at = 0
    for out in sums:
        rows = slice(at, at + out.shape[0])
        at += out.shape[0]
        out[:, :features] = part[rows].astype(out.dtype)
        if out.dtype == F32:
            out[:, features:] = spread[rows]
        else:
            out[:, features:] = wire_pad(spread[rows], experts)


def grads_body(parts, pass_ref, got_ref, acts_ref, *refs):
    gate_hbm, up_hbm, down_hbm, x_ref, scaled_ref, all_ref, gate_ref, up_ref, down_ref, sems = refs
    half, features = pass_ref.shape[0], x_ref.shape[1]
    units = acts_ref.shape[1] // 3
    for i, ref in enumerate((pass_ref, got_ref)):
        rows = pl.ds(i * half, half)
        x_ref[rows, :] = ref[:, :features]
        scaled_ref[rows, :] = ref[:, features : 2 * features]
    all_ref[:half, :] = acts_ref[...]
    all_ref[half:, :] = got_ref[:, 2 * features :]
    step = features // parts
    copies = []
    for i in range(parts):
        at = pl.ds(i * step, step)
        both = contract_first(x_ref[:, at], all_ref[:, units:])
        gate_ref[at, :] = both[:, :units].astype(BF)
        up_ref[at, :] = both[:, units:].astype(BF)
        down_ref[:, at] = contract_first(all_ref[:, :units], scaled_ref[:, at]).astype(BF)
        for j, (src, dst) in enumerate(
            (
                (gate_ref.at[at, :], gate_hbm.at[0, at, :]),
                (up_ref.at[at, :], up_hbm.at[0, at, :]),
                (down_ref.at[:, at], down_hbm.at[0, :, at]),
            )
        ):
            copies.append(pltpu.make_async_copy(src, dst, sems.at[i, j]))
            copies[-1].start()
    for copy in copies:
        copy.wait()


def sum_body(experts, added, stays, *refs):
    keep_ref, parts, outs = refs[0], refs[1 : 1 + added], refs[1 + added :]
    rows, width = outs[0].shape
    for i, out in enumerate(outs):
        at = pl.ds(i * rows, rows)
        total = keep_ref[at, :]
        for part in parts:
            total = total + part[at, :].astype(F32)
        if i == 0 and stays:
            out[...] = total
        else:
            out[:, : width - PAD] = total[:, : width - PAD].astype(BF)
            out[:, width - PAD :] = wire_pad(total[:, width - PAD :], experts)


def sum_parts(keep, parts, pieces, stays, experts, name):
    rows = keep.shape[0] // pieces
    dims = (rows, keep.shape[1])
    outs = [shape(dims, F32 if stays and i == 0 else BF) for i in range(pieces)]
    return call(
        functools.partial(sum_body, experts, len(parts), stays),
        outs,
        name,
        COST if name in LONG else 0,
        1024,
    )(keep, *parts)


def final_body(experts, added, *refs):
    keep_ref, parts, (ids_ref, tokens_ref, gates_ref) = refs[0], refs[1 : 1 + added], refs[1 + added :]
    count, features = tokens_ref.shape
    total = keep_ref[...]
    for part in parts:
        total = total + part[...].astype(F32)
    tokens_ref[...] = total[:, :features].astype(BF)
    product = total[:, features:]
    lane = lanes(count).astype(F32)
    ids = ids_ref[...].astype(F32)
    for k in range(ids.shape[0]):
        id_k = column(ids[k : k + 1])
        picked = (lane == id_k) | (lane == id_k + experts)
        gates_ref[k : k + 1, :] = as_row(
            jnp.sum(jnp.where(picked, product, 0.0), axis=1, keepdims=True)
        )


def to_wire(total, experts):
    pad = total[:, -PAD:]
    rest = jnp.roll(pad - lax.reduce_precision(pad, 8, 7), experts, 1)
    lane = jnp.arange(PAD)[None, :]
    pad = jnp.where((lane >= experts) & (lane < 2 * experts), pad + rest, pad)
    return jnp.concatenate([total[:, :-PAD], pad], axis=1).astype(BF)


def sum_plain(keep, parts, pieces, stays, experts):
    for part in parts:
        keep = keep + part.astype(F32)
    split = jnp.split(keep, pieces, axis=0)
    return [
        piece if stays and i == 0 else to_wire(piece, experts) for i, piece in enumerate(split)
    ]


def expert_plain(pieces, own_slabs, other_slabs, experts, sizes):
    features = own_slabs.shape[0]
    units = own_slabs.shape[1] // 3
    rows = jnp.concatenate(pieces, axis=0)
    rows_x, rows_dy = rows[:, :features], rows[:, features : 2 * features]
    is_own = jnp.arange(PAD, dtype=jnp.int32)[None, :] == lax.axis_index("expert")
    weight = jnp.sum(
        jnp.where(is_own, rows[:, 2 * features :].astype(F32), 0.0), axis=1, keepdims=True
    )
    scaled = (weight * rows_dy.astype(F32)).astype(BF)
    part = product = 0.0
    acts = []
    for slabs in (own_slabs, other_slabs):
        both = jnp.dot(rows_x, slabs[:, : 2 * units], preferred_element_type=F32)
        pre_gate, pre_up = both[:, :units], both[:, units:]
        back = jnp.dot(rows_dy, slabs[:, 2 * units :], preferred_element_type=F32)
        sig = jax.nn.sigmoid(pre_gate)
        active = pre_gate * sig
        hidden = (active * pre_up).astype(BF)
        d_hidden = weight * back
        d_gate = (d_hidden * pre_up * (sig * (1.0 + pre_gate * (1.0 - sig)))).astype(BF)
        d_up = (d_hidden * active).astype(BF)
        product = product + jnp.sum(hidden.astype(F32) * back, axis=1, keepdims=True)
        part = part + contract_last(jnp.concatenate([d_gate, d_up], axis=1), slabs[:, : 2 * units])
        acts.append(jnp.concatenate([hidden, d_gate, d_up], axis=1))
    wide = jnp.concatenate([part, jnp.where(is_own, product, 0.0)], axis=1)
    sums = []
    at = 0
    for rows, dtype in sizes:
        piece = wide[at : at + rows]
        at += rows
        sums.append(piece if dtype == F32 else to_wire(piece, experts))
    return *sums, jnp.concatenate([rows_x, scaled, acts[1]], axis=1), acts[0]


def local(tokens, upstream, route_ids, route_gates, w_gate, w_up, w_down):
    experts = lax.axis_size("expert")
    groups = lax.axis_size("section") // 2
    count, features = tokens.shape
    units = w_gate.shape[2]
    width = features + PAD
    rows = experts * groups * count
    fits = 2 * rows <= LARGEST
    ids, gates = route_ids.T, route_gates.T

    def in_hbm(*values):
        return [pltpu.with_memory_space_constraint(v, pltpu.HBM) for v in values]

    block = pl.pallas_call(
        pack_body,
        out_shape=shape((count, 2 * features + PAD), BF),
        in_specs=[pl.BlockSpec(memory_space=pltpu.HBM)] * 4,
        scratch_shapes=[
            pltpu.VMEM(ids.shape, jnp.int32),
            pltpu.VMEM(ids.shape, BF),
            pltpu.SemaphoreType.DMA((4,)),
        ],
        name="pack",
        compiler_params=pltpu.CompilerParams(vmem_limit_bytes=VMEM),
    )(*in_hbm(tokens, upstream, ids, gates))

    def added(total, parts, pieces, stays, name):
        if fits:
            return sum_parts(total, parts, pieces, stays, experts, name)
        return sum_plain(total, parts, pieces, stays, experts)

    others = sorted(range(1, experts), key=lambda d: -d.bit_count())
    along = [swap(block, "section", 2 * k) for k in range(groups - 1, 1, -1)]
    close = others[::-1]
    near = [swap(block, "expert", d) for d in close]
    far_block = jnp.concatenate(along, axis=0)
    near_block = jnp.concatenate([block] + near, axis=0)

    if fits:
        slabs = pl.pallas_call(
            weights_body,
            out_shape=shape((features, 3 * units), BF),
            in_specs=[pl.BlockSpec(memory_space=pltpu.HBM)] * 3,
            scratch_shapes=[pltpu.VMEM((units, features), BF), pltpu.SemaphoreType.DMA((3,))],
            name="weights",
            compiler_params=pltpu.CompilerParams(vmem_limit_bytes=VMEM),
            cost_estimate=pl.CostEstimate(flops=0, bytes_accessed=1024, transcendentals=0),
        )(*in_hbm(w_gate, w_up, w_down))
    else:
        slabs = jnp.concatenate([w_gate[0], w_up[0], w_down[0].T], axis=1)
    far_block, near_block, slabs = lax.optimization_barrier((far_block, near_block, slabs))
    other_slabs = swap(slabs, "section", 1)

    far = [swap(far_block, "expert", d) for d in others[1:]]
    far += [swap(near_block, "section", 2), swap(far_block, "expert", others[0])]
    *direct, beside, diagonal = far
    pieces = [near_block, far_block, beside, *direct, diagonal]
    sizes = [(experts * count, F32), ((groups - 2) * count, F32), (experts * count, BF)]
    sizes += [((groups - 2) * count, BF)] * len(others)
    if fits:
        back_slabs = call(back_body, shape((4 * units, features), BF), "back")(slabs, other_slabs)
        *split, passed, acts = pl.pallas_call(
            functools.partial(expert_body, experts, len(pieces)),
            out_shape=[shape((size, width), dtype) for size, dtype in sizes]
            + [shape((rows, 2 * features + 3 * units), BF), shape((rows, 3 * units), BF)],
            scratch_shapes=[
                pltpu.VMEM((rows, features), BF),
                pltpu.VMEM((rows, PAD), F32),
            ],
            name="expert",
            compiler_params=pltpu.CompilerParams(vmem_limit_bytes=VMEM),
            cost_estimate=pl.CostEstimate(flops=0, bytes_accessed=1024, transcendentals=0),
        )(*pieces, slabs, other_slabs, back_slabs)
    else:
        *split, passed, acts = expert_plain(pieces, slabs, other_slabs, experts, sizes)

    got = swap(passed, "section", 1)
    if fits:
        grad_gate, grad_up, grad_down = pl.pallas_call(
            functools.partial(grads_body, PARTS),
            out_shape=[shape(w.shape, BF) for w in (w_gate, w_up, w_down)],
            out_specs=[pl.BlockSpec(memory_space=pltpu.HBM)] * 3,
            scratch_shapes=[
                pltpu.VMEM((2 * rows, features), BF),
                pltpu.VMEM((2 * rows, features), BF),
                pltpu.VMEM((2 * rows, 3 * units), BF),
                pltpu.VMEM((features, units), BF),
                pltpu.VMEM((features, units), BF),
                pltpu.VMEM((units, features), BF),
                pltpu.SemaphoreType.DMA((PARTS, 3)),
            ],
            name="grads",
            compiler_params=pltpu.CompilerParams(vmem_limit_bytes=VMEM),
            cost_estimate=pl.CostEstimate(flops=0, bytes_accessed=1024, transcendentals=0),
        )(passed, got, acts)
    else:
        every = jnp.concatenate([passed, got], axis=0)
        acts = jnp.concatenate([acts, got[:, 2 * features :]], axis=0)
        hidden, d_gate, d_up = jnp.split(acts, 3, axis=1)
        rows_x, scaled = every[:, :features], every[:, features : 2 * features]
        grad_gate = contract_first(rows_x, d_gate).astype(BF)[None]
        grad_up = contract_first(rows_x, d_up).astype(BF)[None]
        grad_down = contract_first(hidden, scaled).astype(BF)[None]

    crossed = [
        swap(part, "expert", d) for d, part in zip(others, [split[-1], *split[3:-1]])
    ]
    beside = swap(split[2], "section", 2)
    crossed, grad_gate = lax.optimization_barrier((crossed, grad_gate))
    onward = added(split[1], crossed, groups - 2, False, "sum_far")
    own, *sideways = added(split[0], [beside], experts, True, "sum_near")
    ahead = dict(zip(range(groups - 1, 1, -1), onward))
    along = [swap(ahead[k], "section", 2 * k) for k in range(2, groups)]
    (own,) = added(own, along, 1, True, "sum_along")
    around = dict(zip(close, sideways))
    parts = [swap(around[d], "expert", d) for d in others]
    grad_tokens, grad_gates = call(
        functools.partial(final_body, experts, len(parts)),
        [shape((count, features), BF), shape(ids.shape, F32)],
        "final",
        0,
        4 * count * width * 2,
    )(own, *parts, ids)

    return (
        grad_tokens,
        grad_gates.T,
        grad_gate,
        grad_up,
        grad_down,
    )


def solution(mesh):
    placed = (
        P(("section", "expert"), None),
        P(("section", "expert"), None),
        P(("section", "expert"), None),
        P(("section", "expert"), None),
        P("expert", None, "section"),
        P("expert", None, "section"),
        P("expert", "section", None),
    )
    return jax.shard_map(
        local,
        mesh=mesh,
        in_specs=placed,
        out_specs=(
            P(("section", "expert"), None),
            P(("section", "expert"), None),
            P("expert", None, "section"),
            P("expert", None, "section"),
            P("expert", "section", None),
        ),
        check_vma=False,
    )
```
